512 devices in a mesh: gz: 4 (over z_lo), gy: 4 (over z_hi), gx: 32 (over y, x, core).
Axes of the slice: x: 4, y: 4, z: 16 (z_hi: 4, z_lo: 4; z = z_hi * 4 + z_lo), core: 2. Of those that a mesh axis runs over, the one named last changes fastest.
Arguments:
- section: bfloat16 [4, 1024, 8192], P('gz', 'gy', 'gx'), may hold values from -6 to 6
- first_kernel: float32 [16, 9], replicated, may hold values from -2 to 2
- first_bias: float32 [16], replicated, may hold values from -3 to 3
- second_kernel: bfloat16 [9, 16, 16], replicated, may hold values from -0.5 to 0.5
- second_bias: float32 [16], replicated, may hold values from -3 to 3
- head_weight: float32 [16], replicated, may hold values from -1.5 to 1.5
Outputs:
- spectra: float32 [4, 2, 1024, 8192], P('gz', None, 'gy', 'gx')
The draws below stay inside these ranges and needn't reach their ends.
All inputs are finite; a program needn't handle non-finite values.
Results may differ from the reference program's by a relative error of at most 0.0075.
Values may be sent and summed in bfloat16 or wider, within the bound.
No kernel may reach another device: no remote copies, remote signals or barrier semaphores. Data moves between devices by JAX's collectives and lax.ppermute only.
A program may use at most 128 MiB of HBM per device.

```python
import math
import jax
import jax.numpy as jnp
from jax import lax

CHANNELS = 16
PATCH = 128
ROWS_DEV = 256
COLS_DEV = 256
SECTIONS = 4
HEIGHT = 1024
WIDTH = 8192
N_GY = 4
N_GX = 32


def block_scale(key, extent, cuts, low, largest):
    def one(position, blocks):
        draws = jax.random.uniform(jax.random.fold_in(jax.random.fold_in(key, 6), position), (blocks,), jnp.float32, low / len(cuts), largest / len(cuts))
        return jnp.repeat(jnp.exp(draws), extent[position] // blocks).reshape((-1,) + (1,) * (len(extent) - position - 1))

    level = one(*cuts[0])
    for cut in cuts[1:]:
        level = level * one(*cut)
    return level


def scatter_about(own_key, extent, scale, limit, split=(), kind=jnp.bfloat16):
    array = jax.random.normal(own_key, extent, jnp.float32) * scale
    if len(split) > 0:
        array = block_scale(own_key, extent, split, -0.22, 0.18) * array
    return jnp.clip(array, min=-limit, max=limit).astype(kind)


def setup_inputs(seed: int = 0) -> dict:
    streams_of = jax.random.split(jax.random.key(seed), 7)
    section = scatter_about(streams_of[0], (SECTIONS, HEIGHT, WIDTH), 1.0, 6.0, ((0, 4), (1, 4), (2, 32)))
    first_kernel = scatter_about(streams_of[1], (CHANNELS, 9), 9 ** -0.5, 2.0, (), jnp.float32)
    first_bias = scatter_about(streams_of[2], (CHANNELS,), 0.5, 3.0, (), jnp.float32)
    second_kernel = scatter_about(streams_of[3], (9, CHANNELS, CHANNELS), (9 * CHANNELS) ** -0.5, 0.5)
    second_bias = scatter_about(streams_of[4], (CHANNELS,), 0.5, 3.0, (), jnp.float32)
    head_weight = scatter_about(streams_of[5], (CHANNELS,), CHANNELS ** -0.5, 1.5, (), jnp.float32)
    return {"section": section, "first_kernel": first_kernel, "first_bias": first_bias, "second_kernel": second_kernel, "second_bias": second_bias, "head_weight": head_weight}


def dft_tables(length):
    positions = jnp.arange(length, dtype=jnp.int32)
    phase_step = positions[:, None] * positions[None, :] % length
    angles = phase_step.astype(jnp.float32) * (2.0 * math.pi / length)
    scaling = 1.0 / math.sqrt(length)
    cosine_table = (jnp.cos(angles) * scaling).astype(jnp.bfloat16)
    sine_table = (jnp.sin(angles) * scaling).astype(jnp.bfloat16)
    return (cosine_table, sine_table)

def first_layer(padded, kernel, offsets):
    row_count = padded.shape[0] - 2
    col_count = padded.shape[1] - 2
    values = padded.astype(jnp.float32)
    summed = jnp.zeros((kernel.shape[0], row_count, col_count), jnp.float32)
    for tap_index in range(9):
        row_off = tap_index // 3
        col_off = tap_index % 3
        window = values[row_off:row_off + row_count, col_off:col_off + col_count]
        summed = summed + kernel[:, tap_index][:, None, None] * window[None]
    return jax.nn.relu(summed + offsets[:, None, None]).astype(jnp.bfloat16)

def second_layer(hidden_pad, center, kernel, offsets, head_vec):
    row_count = hidden_pad.shape[1] - 2
    col_count = hidden_pad.shape[2] - 2
    summed = jnp.zeros((kernel.shape[1], row_count, col_count), jnp.float32)
    for tap_index in range(9):
        row_off = tap_index // 3
        col_off = tap_index % 3
        window = hidden_pad[:, row_off:row_off + row_count, col_off:col_off + col_count]
        summed = summed + jnp.einsum('oc,crw->orw', kernel[tap_index].astype(jnp.float32), window.astype(jnp.float32))
    deep = jax.nn.relu(summed + offsets[:, None, None])
    return (center.astype(jnp.float32) + lax.optimization_barrier(jnp.sum(head_vec[:, None, None] * deep, axis=0))).astype(jnp.bfloat16)

def restore_block(padded, first_kernel, first_bias, second_kernel, second_bias, head_weight, row_start, col_start, height, full_width):
    hidden = first_layer(padded, first_kernel, first_bias)
    row_ids = row_start - 1 + jnp.arange(hidden.shape[1], dtype=jnp.int32)
    col_ids = col_start - 1 + jnp.arange(hidden.shape[2], dtype=jnp.int32)
    inside = ((row_ids >= 0) & (row_ids < height))[:, None] & ((col_ids >= 0) & (col_ids < full_width))[None, :]
    hidden = jnp.where(inside[None], hidden, jnp.zeros_like(hidden))
    center = padded[2:-2, 2:-2]
    return second_layer(hidden, center, second_kernel, second_bias, head_weight)

def spectrum(restored, cosine_table, sine_table):
    length = cosine_table.shape[0]
    row_count, col_count = restored.shape
    tiles = restored.reshape(row_count // length, length, col_count // length, length).astype(jnp.float32)
    cos_f = cosine_table.astype(jnp.float32)
    sin_f = sine_table.astype(jnp.float32)
    rows_cos = jnp.einsum('aibj,jk->aibk', tiles, cos_f).astype(jnp.bfloat16).astype(jnp.float32)
    rows_sin = jnp.einsum('aibj,jk->aibk', tiles, sin_f).astype(jnp.bfloat16).astype(jnp.float32)
    real_part = jnp.einsum('ij,aibk->ajbk', cos_f, rows_cos) - jnp.einsum('ij,aibk->ajbk', sin_f, rows_sin)
    imag_part = -(jnp.einsum('ij,aibk->ajbk', cos_f, rows_sin) + jnp.einsum('ij,aibk->ajbk', sin_f, rows_cos))
    return jnp.stack([real_part.reshape(row_count, col_count), imag_part.reshape(row_count, col_count)])

def cross(first_spec, second_spec):
    real_out = first_spec[0] * second_spec[0] + first_spec[1] * second_spec[1]
    imag_out = first_spec[1] * second_spec[0] - first_spec[0] * second_spec[1]
    return jnp.stack([real_out, imag_out])

def reference(section, first_kernel, first_bias, second_kernel, second_bias, head_weight):
    height = ROWS_DEV * N_GY
    full_width = COLS_DEV * N_GX
    block_count = height // ROWS_DEV
    cosine_table, sine_table = dft_tables(PATCH)

    def restore_section(section_image):
        padded = jnp.pad(section_image, 2)

        def one_block(block_index):
            row_start = (block_index * ROWS_DEV).astype(jnp.int32)
            rows_pad = lax.dynamic_slice_in_dim(padded, row_start, ROWS_DEV + 4, 0)
            return restore_block(rows_pad, first_kernel, first_bias, second_kernel, second_bias, head_weight, row_start, jnp.int32(0), height, full_width)
        pieces = lax.map(one_block, jnp.arange(block_count, dtype=jnp.int32))
        return pieces.reshape(height, full_width)
    spectra_list = []
    for sec_index in range(SECTIONS):
        spectra_list.append(spectrum(restore_section(section[sec_index]), cosine_table, sine_table))
    outputs = []
    for sec_index in range(SECTIONS):
        if sec_index + 1 < SECTIONS:
            outputs.append(cross(spectra_list[sec_index], spectra_list[sec_index + 1]))
        else:
            outputs.append(jnp.zeros((2, height, full_width), jnp.float32))
    return jnp.stack(outputs)
```

```python
import math

import jax
import jax.numpy as jnp
import numpy as np
from jax import lax
from jax.experimental import pallas as pl
from jax.experimental.pallas import tpu as pltpu
from jax.sharding import PartitionSpec as P

PATCH = 128
TILE = 256
CH = 16
BAND = 8
BANDS = TILE // BAND
LANES = 128
K1 = 256
K2 = 512
FAR = -65536.0

F32 = jnp.float32
BF16 = jnp.bfloat16
VMEM = pltpu.MemorySpace.VMEM
SMEM = pltpu.MemorySpace.SMEM
PARAMS = pltpu.CompilerParams(vmem_limit_bytes=40 * 1024 * 1024)


def dft_tables():
    positions = np.arange(PATCH, dtype=np.int32)
    phase = positions[:, None] * positions[None, :] % PATCH
    angles = phase.astype(np.float32) * np.float32(2.0 * math.pi / PATCH)
    scaling = np.float32(1.0 / math.sqrt(PATCH))
    cosine = (np.cos(angles) * scaling).astype(BF16)
    sine = (np.sin(angles) * scaling).astype(BF16)
    across = np.concatenate([cosine, sine], axis=1)
    down = np.block([[cosine.T, -sine.T], [-sine.T, -cosine.T]]).astype(BF16)
    return across, down


def iota(shape, dim):
    return lax.broadcasted_iota(jnp.int32, shape, dim)


def dot(a, b):
    return lax.dot_general(a, b, (((1,), (0,)), ((), ())), preferred_element_type=F32)


def pieces(values):
    high = values.astype(BF16)
    rest = values - high.astype(F32)
    middle = rest.astype(BF16)
    low = (rest - middle.astype(F32)).astype(BF16)
    return high, middle, low


def column(row, spread):
    return jnp.sum(jnp.where(spread, row, 0.0), axis=1, keepdims=True)


def prepare_kernel(first_ref, first_bias_ref, second_ref, second_bias_ref, w1_ref, w2_ref):
    rows = BAND * CH
    row_r = iota((rows, K1), 0) // CH
    col = iota((rows, K1), 1)
    col_i = col % 16
    col_k = col - 240
    stacked = jnp.concatenate(pieces(first_ref[...]), axis=0)
    spread = (iota((rows, 48), 0) % CH == iota((rows, 48), 1) % CH).astype(BF16)
    sel_t = iota((9, K1), 0)
    sel_col = iota((9, K1), 1)
    sel_s = sel_col % 80 // 16
    own_piece = iota((48, K1), 0) // CH == iota((48, K1), 1) // 80
    spread_bias = iota((rows, CH), 0) % CH == iota((rows, CH), 1)
    bias = [column(p.astype(F32), spread_bias) for p in pieces(first_bias_ref[...])]
    for dw in range(3):
        total = jnp.zeros((rows, K1), F32)
        for a in range(3):
            b = sel_s - dw
            select = (sel_t == 3 * a + b) & (b >= 0) & (b <= 2) & (sel_col < 240)
            picked = dot(stacked, select.astype(F32).astype(BF16))
            picked = jnp.where(own_piece, picked, 0.0).astype(BF16)
            total = total + jnp.where(col_i - row_r == a, dot(spread, picked), 0.0)
        total = jnp.where(col >= 240, 0.0, total)
        for k in range(3):
            total = jnp.where(col_k == k, bias[k], total)
        if dw == 0:
            total = jnp.where(col_k == 3, FAR, total)
        if dw == 2:
            total = jnp.where(col_k == 4, FAR, total)
        total = jnp.where((col_k == 5) & (row_r < 7), FAR, total)
        total = jnp.where((col_k == 6) & (row_r == 7), FAR, total)
        w1_ref[dw * rows : (dw + 1) * rows, :] = total.astype(BF16)
    rows = CH * BAND
    row_r = iota((rows, K2), 0) % BAND
    col = iota((rows, K2), 1)
    col_r = col % 160 // CH
    spread = (iota((rows, CH), 0) // BAND == iota((rows, CH), 1)).astype(BF16)
    f_c = iota((CH, K2), 0)
    f_col = iota((CH, K2), 1)
    total = jnp.zeros((rows, K2), F32)
    for a in range(3):
        picked = jnp.zeros((CH, K2), F32)
        for dw in range(3):
            place = (f_col // 160 == dw) & (f_col % CH == f_c)
            picked = picked + dot(second_ref[3 * a + dw], place.astype(F32).astype(BF16))
        total = total + jnp.where(col_r - row_r == a, dot(spread, picked.astype(BF16)), 0.0)
    total = jnp.where(col >= 480, 0.0, total)
    spread_bias = iota((rows, CH), 0) // BAND == iota((rows, CH), 1)
    for k, piece in enumerate(pieces(second_bias_ref[...])):
        total = jnp.where(col == 480 + k, column(piece.astype(F32), spread_bias), total)
    w2_ref[...] = total.astype(BF16)


def shifted(left, own, right):
    wide = jnp.concatenate([left, own, right], axis=1)
    return [wide[:, LANES - 2 + s : LANES - 2 + s + TILE] for s in range(5)]


def edge_rows(flags_ref, top, bottom):
    row = iota((16, TILE), 0)
    lane = iota((16, TILE), 1)
    keep = row < 3
    keep = keep | ((row == 3) & (lane == 0) & (flags_ref[0] > 0))
    keep = keep | ((row == 4) & (lane == TILE - 1) & (flags_ref[1] > 0))
    if top:
        keep = keep | ((row == 5) & (flags_ref[2] > 0))
    if bottom:
        keep = keep | ((row == 6) & (flags_ref[3] > 0))
    return jnp.where(keep, 1.0, 0.0).astype(BF16)


def ones_rows():
    return jnp.where(iota((16, TILE), 0) < 3, 1.0, 0.0).astype(BF16)


def hidden_band(w1, shifts, last_rows):
    raw = [x.astype(BF16) for x in shifts]
    grid = jnp.concatenate(raw * 3 + [last_rows], axis=0)
    return jnp.maximum(dot(w1, grid), 0.0).astype(BF16)


def restored_band(w2, hidden, ones, head_ref, center):
    deep = dot(w2, jnp.concatenate(hidden + [ones, jnp.zeros((16, TILE), BF16)], axis=0))
    total = center
    parts = [head_ref[o] * jnp.maximum(deep[o * BAND : (o + 1) * BAND], 0.0) for o in range(CH)]
    while len(parts) > 1:
        parts = [parts[i] + parts[i + 1] for i in range(0, len(parts), 2)]
    return center + parts[0]


def inner_kernel(
    flags_ref, head_ref, left_ref, own_ref, right_ref, w1_ref, w2_ref, out_ref, raw_ref, hid_ref, res_ref
):
    band_rows = BAND * CH
    for r in range(0, TILE, 16):
        own = own_ref[r : r + 16, :].astype(F32)
        left = left_ref[r : r + 16, :].astype(F32)
        right = right_ref[r : r + 16, :].astype(F32)
        for s, x in enumerate(shifted(left, own, right)):
            raw_ref[s, r : r + 16, :] = x
    ones = ones_rows()
    last_rows = edge_rows(flags_ref, False, False)

    def first(j):
        start = pl.multiple_of((j - 1) * BAND, BAND)
        return hidden_band(
            w1_ref[...], [raw_ref[s, pl.ds(start, 16), :] for s in range(5)], last_rows
        )

    def keep(j, hidden):
        start = pl.multiple_of(j * band_rows, band_rows)
        for dw in range(3):
            hid_ref[dw, pl.ds(start, band_rows), :] = hidden[dw * band_rows : (dw + 1) * band_rows]

    def second(b):
        start = pl.multiple_of((b * BAND + 6) * CH, CH)
        hidden = [hid_ref[dw, pl.ds(start, 160), :] for dw in range(3)]
        center_start = pl.multiple_of(b * BAND, BAND)
        res_ref[pl.ds(center_start, BAND), :] = restored_band(
            w2_ref[...], hidden, ones, head_ref, raw_ref[2, pl.ds(center_start, BAND), :]
        )

    keep(1, first(1))
    keep(2, first(2))

    def body(j, carry):
        second(j - 2)
        keep(j, first(j))
        return carry

    lax.fori_loop(3, BANDS, body, 0, unroll=UNROLL)
    second(BANDS - 2)
    res_ref[0:BAND, :] = jnp.zeros((BAND, TILE), F32)
    res_ref[TILE - BAND :, :] = jnp.zeros((BAND, TILE), F32)
    out_ref[...] = res_ref[...].astype(BF16)


UNROLL = 2


def outer_kernel(
    flags_ref, head_ref, left_ref, own_ref, right_ref, above_ref, below_ref, w1_ref, w2_ref, inner_ref, out_ref
):
    band_rows = BAND * CH
    ones = ones_rows()
    out_ref[16 : TILE - 16, :] = inner_ref[16 : TILE - 16, :]
    for top in (True, False):
        if top:
            near = slice(0, 16)
            far = above_ref[...].astype(F32)[8:16]
        else:
            near = slice(TILE - 16, TILE)
            far = below_ref[...].astype(F32)[0:8]
        own = own_ref[near, :].astype(F32)
        parts = [left_ref[near, :].astype(F32), own, right_ref[near, :].astype(F32)]
        halo = [far[:, :LANES], far[:, LANES : LANES + TILE], far[:, LANES + TILE :]]
        order = (halo, parts) if top else (parts, halo)
        shifts = shifted(*[jnp.concatenate([u, v], axis=0) for u, v in zip(*order)])
        blocks = [
            hidden_band(
                w1_ref[...],
                [x[8 * k : 8 * k + 16] for x in shifts],
                edge_rows(flags_ref, top and k == 0, not top and k == 1),
            )
            for k in range(2)
        ]
        hidden = [
            jnp.concatenate([blk[dw * band_rows : (dw + 1) * band_rows] for blk in blocks], axis=0)[96:]
            for dw in range(3)
        ]
        center = own[0:8] if top else own[8:16]
        band = restored_band(w2_ref[...], hidden, ones, head_ref, center)
        inner = inner_ref[near, :].astype(F32)
        pair = [band, inner[8:16]] if top else [inner[0:8], band]
        out_ref[near, :] = jnp.concatenate(pair, axis=0).astype(BF16)


def transform(image_ref, across_ref, down_ref):
    halves = [
        dot(image_ref[:, q * PATCH : (q + 1) * PATCH], across_ref[...]).astype(BF16) for q in range(2)
    ]
    real, imag = [], []
    for a in range(2):
        rows = slice(a * PATCH, (a + 1) * PATCH)
        cos_rows = jnp.concatenate([h[rows, :PATCH] for h in halves], axis=1)
        sin_rows = jnp.concatenate([h[rows, PATCH:] for h in halves], axis=1)
        both = dot(down_ref[...], jnp.concatenate([cos_rows, sin_rows], axis=0))
        real.append(both[:PATCH])
        imag.append(both[PATCH:])
    return real, imag


def own_kernel(image_ref, across_ref, down_ref, out_ref):
    real, imag = transform(image_ref, across_ref, down_ref)
    for a in range(2):
        rows = slice(a * PATCH, (a + 1) * PATCH)
        out_ref[0, rows, :] = real[a]
        out_ref[1, rows, :] = imag[a]


def cross_kernel(image_ref, across_ref, down_ref, own_ref, out_ref):
    real, imag = transform(image_ref, across_ref, down_ref)
    for a in range(2):
        rows = slice(a * PATCH, (a + 1) * PATCH)
        own_real, own_imag = own_ref[0, rows, :], own_ref[1, rows, :]
        out_ref[0, 0, rows, :] = own_real * real[a] + own_imag * imag[a]
        out_ref[0, 1, rows, :] = own_imag * real[a] - own_real * imag[a]


def full(shape):
    return pl.BlockSpec(shape, lambda i: (0,) * len(shape), memory_space=VMEM)


def smem():
    return pl.BlockSpec(memory_space=SMEM)


LEFT = pl.BlockSpec((TILE, LANES), lambda i: (0, 1), memory_space=VMEM)
RIGHT = pl.BlockSpec((TILE, LANES), lambda i: (0, 0), memory_space=VMEM)


def call(kernel, name, out_shape, in_specs, scratch=(), flops=0):
    return pl.pallas_call(
        kernel,
        name=name,
        grid=(1,),
        out_shape=out_shape,
        in_specs=in_specs,
        out_specs=jax.tree.map(lambda o: full(o.shape), out_shape),
        scratch_shapes=list(scratch),
        compiler_params=PARAMS,
        cost_estimate=pl.CostEstimate(flops=flops, bytes_accessed=1 << 20, transcendentals=0),
    )


def prepare(first_kernel, first_bias, second_kernel, second_bias):
    return call(
        prepare_kernel,
        "weights",
        (jax.ShapeDtypeStruct((3 * BAND * CH, K1), BF16), jax.ShapeDtypeStruct((CH * BAND, K2), BF16)),
        [full((CH, 9)), full((1, CH)), full((9, CH, CH)), full((1, CH))],
        flops=1 << 28,
    )(first_kernel, first_bias[None], second_kernel, second_bias[None])


TILE_SHAPE = jax.ShapeDtypeStruct((TILE, TILE), BF16)
W_SPECS = [full((3 * BAND * CH, K1)), full((CH * BAND, K2))]


def inner(flags, head, left, own, right, w1, w2):
    return call(
        inner_kernel,
        "inner_rows",
        TILE_SHAPE,
        [smem(), smem(), LEFT, full((TILE, TILE)), RIGHT] + W_SPECS,
        scratch=[
            pltpu.VMEM((5, TILE, TILE), F32),
            pltpu.VMEM((3, (BANDS + 1) * BAND * CH, TILE), BF16),
            pltpu.VMEM((TILE, TILE), F32),
        ],
        flops=3 << 30,
    )(flags, head, left, own, right, w1, w2)


def outer(flags, head, left, own, right, above, below, w1, w2, inside):
    return call(
        outer_kernel,
        "outer_rows",
        TILE_SHAPE,
        [smem(), smem(), LEFT, full((TILE, TILE)), RIGHT]
        + [full((16, TILE + 2 * LANES))] * 2
        + W_SPECS
        + [full((TILE, TILE))],
        flops=1 << 28,
    )(flags, head, left, own, right, above, below, w1, w2, inside)


def table_specs():
    return [full((TILE, TILE)), full((PATCH, 2 * PATCH)), full((2 * PATCH, 2 * PATCH))]


def own_spectrum(image, across, down):
    return call(
        own_kernel,
        "own_spectrum",
        jax.ShapeDtypeStruct((2, TILE, TILE), F32),
        table_specs(),
        flops=1 << 29,
    )(image, across, down)


def cross_spectrum(image, across, down, own):
    return call(
        cross_kernel,
        "cross_spectrum",
        jax.ShapeDtypeStruct((1, 2, TILE, TILE), F32),
        table_specs() + [full((2, TILE, TILE))],
        flops=1 << 29,
    )(image, across, down, own)


def from_step(value, axis, step):
    count = lax.axis_size(axis)
    pairs = [(i, i + step) for i in range(count) if 0 <= i + step < count]
    return lax.ppermute(value, axis, pairs)


def on_device(section, first_kernel, first_bias, second_kernel, second_bias, head_weight):
    own = section[0]
    gx, gy = lax.axis_index("gx"), lax.axis_index("gy")
    ends = [gx == 0, gx == lax.axis_size("gx") - 1, gy == 0, gy == lax.axis_size("gy") - 1]
    flags = jnp.stack(ends).astype(jnp.int32)
    left = from_step(own, "gx", 1)
    right = from_step(own, "gx", -1)
    w1, w2 = prepare(first_kernel, first_bias, second_kernel, second_bias)

    def slab(rows):
        return jnp.concatenate([left[rows, LANES:], own[rows], right[rows, :LANES]], axis=1)

    above = from_step(slab(slice(TILE - 16, TILE)), "gy", 1)
    below = from_step(slab(slice(0, 16)), "gy", -1)
    inside = inner(flags, head_weight, left, own, right, w1, w2)
    restored = outer(flags, head_weight, left, own, right, above, below, w1, w2, inside)
    across, down = dft_tables()
    later = from_step(restored, "gz", -1)
    spectrum = own_spectrum(restored, across, down)
    return cross_spectrum(later, across, down, spectrum)


def solution(mesh):
    placed = (P("gz", "gy", "gx"), P(), P(), P(), P(), P())
    return jax.shard_map(
        on_device, mesh=mesh, in_specs=placed, out_specs=P("gz", None, "gy", "gx"), check_vma=False
    )
```

```python
import math

import jax
import jax.numpy as jnp
import numpy as np
from jax import lax
from jax.experimental import pallas as pl
from jax.experimental.pallas import tpu as pltpu
from jax.sharding import PartitionSpec as P

PATCH = 128
TILE = 256
CH = 16
BAND = 8
BANDS = TILE // BAND
LANES = 128
K1 = 256
K2 = 512
FAR = -65536.0

F32 = jnp.float32
BF16 = jnp.bfloat16
VMEM = pltpu.MemorySpace.VMEM
SMEM = pltpu.MemorySpace.SMEM
PARAMS = pltpu.CompilerParams(vmem_limit_bytes=40 * 1024 * 1024)


def dft_tables():
    positions = np.arange(PATCH, dtype=np.int32)
    phase = positions[:, None] * positions[None, :] % PATCH
    angles = phase.astype(np.float32) * np.float32(2.0 * math.pi / PATCH)
    scaling = np.float32(1.0 / math.sqrt(PATCH))
    cosine = (np.cos(angles) * scaling).astype(BF16)
    sine = (np.sin(angles) * scaling).astype(BF16)
    across = np.concatenate([cosine, sine], axis=1)
    down = np.block([[cosine.T, -sine.T], [-sine.T, -cosine.T]]).astype(BF16)
    return across, down


def iota(shape, dim):
    return lax.broadcasted_iota(jnp.int32, shape, dim)


def dot(a, b):
    return lax.dot_general(a, b, (((1,), (0,)), ((), ())), preferred_element_type=F32)


def pieces(values):
    high = values.astype(BF16)
    rest = values - high.astype(F32)
    middle = rest.astype(BF16)
    low = (rest - middle.astype(F32)).astype(BF16)
    return high, middle, low


def column(row, spread):
    return jnp.sum(jnp.where(spread, row, 0.0), axis=1, keepdims=True)


def end_of(axis, last):
    return lax.axis_index(axis) == (lax.axis_size(axis) - 1 if last else 0)


def first_weights_kernel(first_ref, bias_ref, w1_ref, rows_out):
    rows = BAND * CH
    row_r = iota((rows, K1), 0) // CH
    col = iota((rows, K1), 1)
    col_i = col % 16
    stacked = jnp.concatenate(pieces(first_ref[...]), axis=0)
    spread = (iota((rows, 48), 0) % CH == iota((rows, 48), 1) % CH).astype(F32).astype(BF16)
    sel_t = iota((9, K1), 0)
    sel_col = iota((9, K1), 1)
    sel_b = sel_col % 80 // 16
    in_grid = (sel_b <= 2) & (sel_col < 240)
    own_piece = iota((48, K1), 0) // CH == iota((48, K1), 1) // 80
    base = jnp.zeros((rows, K1), F32)
    for a in range(3):
        select = (sel_t == 3 * a + sel_b) & in_grid
        picked = dot(stacked, select.astype(F32).astype(BF16))
        picked = jnp.where(own_piece, picked, 0.0).astype(BF16)
        base = base + jnp.where(col_i - row_r == a, dot(spread, picked), 0.0)
    spread_bias = iota((rows, CH), 0) % CH == iota((rows, CH), 1)
    tail = jnp.zeros((rows, K1), F32)
    for k, piece in enumerate(pieces(bias_ref[...])):
        tail = jnp.where(col == 240 + k, column(piece.astype(F32), spread_bias), tail)
    tail = jnp.where((col == 245) & (row_r < 7), FAR, tail)
    tail = jnp.where((col == 246) & (row_r == 7), FAR, tail)
    for dw in range(3):
        total = jnp.where(col < 240, pltpu.roll(base, 16 * dw, 1) if dw else base, tail)
        if dw == 0:
            total = jnp.where(col == 243, FAR, total)
        if dw == 2:
            total = jnp.where(col == 244, FAR, total)
        w1_ref[dw * rows : (dw + 1) * rows, :] = total.astype(BF16)
    row = iota((16, TILE), 0)
    lane = iota((16, TILE), 1)
    keep = row < 3
    keep = keep | ((row == 3) & (lane == 0) & end_of("gx", False))
    keep = keep | ((row == 4) & (lane == TILE - 1) & end_of("gx", True))
    top = keep | ((row == 5) & end_of("gy", False))
    bottom = keep | ((row == 6) & end_of("gy", True))
    for k, mask in enumerate((keep, top, bottom)):
        rows_out[16 * k : 16 * k + 16, :] = jnp.where(mask, 1.0, 0.0).astype(BF16)


def second_weights_kernel(second_ref, bias_ref, head_ref, w2_ref, head_out):
    rows = CH * BAND
    row_r = iota((rows, K2), 0) % BAND
    col = iota((rows, K2), 1)
    col_r = col % 160 // CH
    spread = (iota((rows, CH), 0) // BAND == iota((rows, CH), 1)).astype(F32).astype(BF16)
    f_c = iota((CH, K2), 0)
    f_col = iota((CH, K2), 1)
    second = second_ref[...].reshape(9 * CH, CH)
    by_dw = [
        dot(second, ((f_col // 160 == dw) & (f_col % CH == f_c)).astype(F32).astype(BF16)) for dw in range(3)
    ]
    total = jnp.zeros((rows, K2), F32)
    for a in range(3):
        picked = sum(by_dw[dw][(3 * a + dw) * CH : (3 * a + dw + 1) * CH] for dw in range(3))
        total = total + jnp.where(col_r - row_r == a, dot(spread, picked.astype(BF16)), 0.0)
    total = jnp.where(col >= 480, 0.0, total)
    spread_bias = iota((rows, CH), 0) // BAND == iota((rows, CH), 1)
    for k, piece in enumerate(pieces(bias_ref[...])):
        total = jnp.where(col == 480 + k, column(piece.astype(F32), spread_bias), total)
    w2_ref[...] = total.astype(BF16)
    head_out[...] = jnp.broadcast_to(column(head_ref[...], spread_bias), (rows, LANES))


def sides_kernel(own_ref, core_ref, chip_ref, sides_ref, head_ref, tail_ref):
    odd = lax.axis_index("gx") % 2 == 1
    for r in range(0, TILE, 16):
        core, chip, own = core_ref[r : r + 16, :], chip_ref[r : r + 16, :], own_ref[r : r + 16, :]
        left = jnp.where(odd, core[:, LANES:], chip[:, LANES:])
        right = jnp.where(odd, chip[:, :LANES], core[:, :LANES])
        sides_ref[r : r + 16, :] = jnp.concatenate([left, right], axis=1)
        if r == 0:
            head_ref[...] = jnp.concatenate([left, own, right], axis=1)
        if r == TILE - 16:
            tail_ref[...] = jnp.concatenate([left, own, right], axis=1)


def shifted(left, own, right):
    wide = jnp.concatenate([left, own, right], axis=1)
    return [wide[:, LANES - 2 + s : LANES - 2 + s + TILE] for s in range(5)]


def ones_rows():
    return jnp.where(iota((16, TILE), 0) < 3, 1.0, 0.0).astype(BF16)


def hidden_band(w1, shifts, last_rows):
    raw = [x.astype(BF16) for x in shifts]
    grid = jnp.concatenate(raw * 3 + [last_rows], axis=0)
    return jnp.maximum(dot(w1, grid), 0.0).astype(BF16)


def restored_band(w2, hidden, ones, head, center):
    deep = dot(w2, jnp.concatenate(hidden + [ones, jnp.zeros((16, TILE), BF16)], axis=0))
    deep = jnp.maximum(deep, 0.0) * jnp.concatenate([head, head], axis=1)
    parts = [deep[o * BAND : (o + 1) * BAND] for o in range(CH)]
    while len(parts) > 1:
        parts = [parts[i] + parts[i + 1] for i in range(0, len(parts), 2)]
    return center + parts[0]


def inner_kernel(
    own_ref, sides_ref, w1_ref, w2_ref, head_ref, rows_ref, out_ref, raw_ref, hid_ref, res_ref
):
    band_rows = BAND * CH
    for r in range(0, TILE, 16):
        own = own_ref[r : r + 16, :].astype(F32)
        left = sides_ref[r : r + 16, :LANES].astype(F32)
        right = sides_ref[r : r + 16, LANES:].astype(F32)
        for s, x in enumerate(shifted(left, own, right)):
            raw_ref[s, r : r + 16, :] = x
    ones = ones_rows()
    last_rows = rows_ref[0:16, :]

    def first(j):
        start = pl.multiple_of((j - 1) * BAND, BAND)
        return hidden_band(
            w1_ref[...], [raw_ref[s, pl.ds(start, 16), :] for s in range(5)], last_rows
        )

    def keep(j, hidden):
        start = pl.multiple_of(j * band_rows, band_rows)
        for dw in range(3):
            hid_ref[dw, pl.ds(start, band_rows), :] = hidden[dw * band_rows : (dw + 1) * band_rows]

    def second(b):
        start = pl.multiple_of((b * BAND + 6) * CH, CH)
        hidden = [hid_ref[dw, pl.ds(start, 160), :] for dw in range(3)]
        center_start = pl.multiple_of(b * BAND, BAND)
        res_ref[pl.ds(center_start, BAND), :] = restored_band(
            w2_ref[...], hidden, ones, head_ref[...], raw_ref[2, pl.ds(center_start, BAND), :]
        )

    def body1(j, carry):
        keep(j, first(j))
        return carry

    def body2(b, carry):
        second(b)
        return carry

    lax.fori_loop(1, BANDS, body1, 0, unroll=UNROLL)
    lax.fori_loop(1, BANDS - 1, body2, 0, unroll=UNROLL2)
    res_ref[0:BAND, :] = jnp.zeros((BAND, TILE), F32)
    res_ref[TILE - BAND :, :] = jnp.zeros((BAND, TILE), F32)
    out_ref[...] = res_ref[...].astype(BF16)


UNROLL = 31
UNROLL2 = 30


def outer_kernel(
    own_ref, sides_ref, below_ref, above_ref, w1_ref, w2_ref, head_ref, rows_ref, inner_ref, out_ref
):
    band_rows = BAND * CH
    ones = ones_rows()
    out_ref[16 : TILE - 16, :] = inner_ref[16 : TILE - 16, :]
    for top in (True, False):
        if top:
            near = slice(0, 16)
            far = above_ref[...].astype(F32)[8:16]
        else:
            near = slice(TILE - 16, TILE)
            far = below_ref[...].astype(F32)[0:8]
        own = own_ref[near, :].astype(F32)
        parts = [sides_ref[near, :LANES].astype(F32), own, sides_ref[near, LANES:].astype(F32)]
        halo = [far[:, :LANES], far[:, LANES : LANES + TILE], far[:, LANES + TILE :]]
        order = (halo, parts) if top else (parts, halo)
        shifts = shifted(*[jnp.concatenate([u, v], axis=0) for u, v in zip(*order)])
        blocks = []
        for k in range(2):
            kind = 1 if top and k == 0 else 2 if k == 1 and not top else 0
            last_rows = rows_ref[16 * kind : 16 * kind + 16, :]
            blocks.append(hidden_band(w1_ref[...], [x[8 * k : 8 * k + 16] for x in shifts], last_rows))
        hidden = [
            jnp.concatenate([blk[dw * band_rows : (dw + 1) * band_rows] for blk in blocks], axis=0)[96:]
            for dw in range(3)
        ]
        center = own[0:8] if top else own[8:16]
        band = restored_band(w2_ref[...], hidden, ones, head_ref[...], center)
        inner = inner_ref[near, :].astype(F32)
        pair = [band, inner[8:16]] if top else [inner[0:8], band]
        out_ref[near, :] = jnp.concatenate(pair, axis=0).astype(BF16)


def transform(image_ref, across_ref, down_ref):
    halves = [
        dot(image_ref[:, q * PATCH : (q + 1) * PATCH], across_ref[...]).astype(BF16) for q in range(2)
    ]
    results = []
    for a in range(2):
        rows = slice(a * PATCH, (a + 1) * PATCH)
        cos_rows = jnp.concatenate([h[rows, :PATCH] for h in halves], axis=1)
        sin_rows = jnp.concatenate([h[rows, PATCH:] for h in halves], axis=1)
        both = dot(down_ref[...], jnp.concatenate([cos_rows, sin_rows], axis=0))
        results.append((both[:PATCH], both[PATCH:]))
    return results


def own_kernel(image_ref, across_ref, down_ref, out_ref):
    for a, (real, imag) in enumerate(transform(image_ref, across_ref, down_ref)):
        rows = slice(a * PATCH, (a + 1) * PATCH)
        out_ref[0, rows, :] = real
        out_ref[1, rows, :] = imag


def cross_kernel(image_ref, across_ref, down_ref, own_ref, out_ref, held_ref, sems):
    copies = []
    for a, (real, imag) in enumerate(transform(image_ref, across_ref, down_ref)):
        rows = slice(a * PATCH, (a + 1) * PATCH)
        own_real, own_imag = own_ref[0, rows, :], own_ref[1, rows, :]
        for part, value in enumerate(
            (own_real * real + own_imag * imag, own_imag * real - own_real * imag)
        ):
            held_ref[part, rows, :] = value
            copies.append(
                pltpu.make_async_copy(held_ref.at[part, rows], out_ref.at[0, part, rows], sems.at[a, part])
            )
            copies[-1].start()
    for copy in copies:
        copy.wait()


def full(shape):
    return pl.BlockSpec(shape, lambda: (0,) * len(shape), memory_space=VMEM)


def call(kernel, name, out_shape, args, scratch=(), flops=0, in_specs=None, out_specs=None):
    return pl.pallas_call(
        kernel,
        name=name,
        out_shape=out_shape,
        in_specs=in_specs or [full(a.shape) for a in args],
        out_specs=out_specs or jax.tree.map(lambda o: full(o.shape), out_shape),
        scratch_shapes=list(scratch),
        compiler_params=PARAMS,
        cost_estimate=pl.CostEstimate(flops=flops, bytes_accessed=1 << 20, transcendentals=0),
    )(*args)


def shaped(*shape, dtype=BF16):
    return jax.ShapeDtypeStruct(shape, dtype)


def prepare(first_kernel, first_bias, second_kernel, second_bias, head):
    w2, head = call(
        second_weights_kernel,
        "second_weights",
        (shaped(CH * BAND, K2), shaped(CH * BAND, LANES, dtype=F32)),
        (second_kernel, second_bias[None], head[None]),
        flops=1 << 31,
    )
    w1, rows = call(
        first_weights_kernel,
        "first_weights",
        (shaped(3 * BAND * CH, K1), shaped(48, TILE)),
        (first_kernel, first_bias[None]),
        flops=1 << 31,
    )
    return w1, w2, head, rows


def sides(own, core, chip):
    slab = shaped(16, TILE + 2 * LANES)
    return call(sides_kernel, "sides", (shaped(TILE, TILE), slab, slab), (own, core, chip), flops=1 << 26)


def inner(own, side, weights):
    return call(
        inner_kernel,
        "inner_rows",
        shaped(TILE, TILE),
        (own, side, *weights),
        scratch=[
            pltpu.VMEM((5, TILE, TILE), F32),
            pltpu.VMEM((3, (BANDS + 1) * BAND * CH, TILE), BF16),
            pltpu.VMEM((TILE, TILE), F32),
        ],
        flops=3 << 30,
    )


def outer(own, side, above, below, weights, inside):
    return call(
        outer_kernel,
        "outer_rows",
        shaped(TILE, TILE),
        (own, side, below, above, *weights, inside),
        flops=1 << 28,
    )


def own_spectrum(image, across, down):
    return call(
        own_kernel, "own_spectrum", shaped(2, TILE, TILE, dtype=F32), (image, across, down), flops=1 << 29
    )


def cross_spectrum(image, across, down, own):
    return call(
        cross_kernel,
        "cross_spectrum",
        shaped(1, 2, TILE, TILE, dtype=F32),
        (image, across, down, own),
        scratch=[pltpu.VMEM((2, TILE, TILE), F32), pltpu.SemaphoreType.DMA((2, 2))],
        flops=1 << 29,
        out_specs=pl.BlockSpec(memory_space=pl.ANY),
    )


def from_step(value, axis, step):
    count = lax.axis_size(axis)
    pairs = [(i, i + step) for i in range(count) if 0 <= i + step < count]
    return lax.ppermute(value, axis, pairs)


def swap(value, axis, offset):
    count = lax.axis_size(axis)
    pairs = [(i, i + 1) for i in range(offset, count - 1, 2)]
    return lax.ppermute(value, axis, pairs + [(j, i) for i, j in pairs])


def on_device(section, first_kernel, first_bias, second_kernel, second_bias, head_weight):
    own = section[0]
    chip = swap(own, "gx", 1)
    core = swap(own, "gx", 0)
    weights = prepare(first_kernel, first_bias, second_kernel, second_bias, head_weight)
    side, head, tail = sides(own, core, chip)
    below = from_step(head, "gy", -1)
    above = from_step(tail, "gy", 1)
    inside = inner(own, side, weights)
    restored = outer(own, side, above, below, weights, inside)
    across, down = dft_tables()
    later = from_step(restored, "gz", -1)
    spectrum = own_spectrum(restored, across, down)
    return cross_spectrum(later, across, down, spectrum)


def solution(mesh):
    placed = (P("gz", "gy", "gx"), P(), P(), P(), P(), P())
    return jax.shard_map(
        on_device, mesh=mesh, in_specs=placed, out_specs=P("gz", None, "gy", "gx"), check_vma=False
    )
```

```python
import math

import jax
import jax.numpy as jnp
import numpy as np
from jax import lax
from jax.experimental import pallas as pl
from jax.experimental.pallas import tpu as pltpu
from jax.sharding import PartitionSpec as P

PATCH = 128
TILE = 256
CH = 16
BAND = 8
BANDS = TILE // BAND
LANES = 128
K1 = 256
K2 = 512
FAR = -65536.0

F32 = jnp.float32
BF16 = jnp.bfloat16
VMEM = pltpu.MemorySpace.VMEM
SMEM = pltpu.MemorySpace.SMEM
PARAMS = pltpu.CompilerParams(vmem_limit_bytes=40 * 1024 * 1024)


def dft_tables():
    positions = np.arange(PATCH, dtype=np.int32)
    phase = positions[:, None] * positions[None, :] % PATCH
    angles = phase.astype(np.float32) * np.float32(2.0 * math.pi / PATCH)
    scaling = np.float32(1.0 / math.sqrt(PATCH))
    cosine = (np.cos(angles) * scaling).astype(BF16)
    sine = (np.sin(angles) * scaling).astype(BF16)
    across = np.concatenate([cosine, sine], axis=1)
    down = np.block([[cosine.T, -sine.T], [-sine.T, -cosine.T]]).astype(BF16)
    return across, down


def iota(shape, dim):
    return lax.broadcasted_iota(jnp.int32, shape, dim)


def dot(a, b):
    return lax.dot_general(a, b, (((1,), (0,)), ((), ())), preferred_element_type=F32)


def pieces(values):
    high = values.astype(BF16)
    rest = values - high.astype(F32)
    middle = rest.astype(BF16)
    low = (rest - middle.astype(F32)).astype(BF16)
    return high, middle, low


def column(row, spread):
    return jnp.sum(jnp.where(spread, row, 0.0), axis=1, keepdims=True)


def end_of(axis, last):
    return lax.axis_index(axis) == (lax.axis_size(axis) - 1 if last else 0)


def waits():
    return lax.axis_index("gy") > 0


def last_rows_kernel(rows_out):
    row = iota((16, TILE), 0)
    lane = iota((16, TILE), 1)
    keep = row < 3
    keep = keep | ((row == 3) & (lane == 0) & end_of("gx", False))
    keep = keep | ((row == 4) & (lane == TILE - 1) & end_of("gx", True))
    top = keep | ((row == 5) & end_of("gy", False))
    bottom = keep | ((row == 6) & end_of("gy", True))
    for k, mask in enumerate((keep, top, bottom)):
        rows_out[16 * k : 16 * k + 16, :] = jnp.where(mask, 1.0, 0.0).astype(BF16)


def first_weights(first_ref, bias_ref, rows_ref, w1_ref, rows_out):
    rows = BAND * CH
    row_r = iota((rows, K1), 0) // CH
    col = iota((rows, K1), 1)
    col_i = col % 16
    stacked = jnp.concatenate(pieces(first_ref[...]), axis=0)
    spread = (iota((rows, 48), 0) % CH == iota((rows, 48), 1) % CH).astype(F32).astype(BF16)
    sel_t = iota((9, K1), 0)
    sel_col = iota((9, K1), 1)
    sel_b = sel_col % 80 // 16
    in_grid = (sel_b <= 2) & (sel_col < 240)
    own_piece = iota((48, K1), 0) // CH == iota((48, K1), 1) // 80
    base = jnp.zeros((rows, K1), F32)
    for a in range(3):
        select = (sel_t == 3 * a + sel_b) & in_grid
        picked = dot(stacked, select.astype(F32).astype(BF16))
        picked = jnp.where(own_piece, picked, 0.0).astype(BF16)
        base = base + jnp.where(col_i - row_r == a, dot(spread, picked), 0.0)
    spread_bias = iota((rows, CH), 0) % CH == iota((rows, CH), 1)
    tail = jnp.zeros((rows, K1), F32)
    for k, piece in enumerate(pieces(bias_ref[...])):
        tail = jnp.where(col == 240 + k, column(piece.astype(F32), spread_bias), tail)
    tail = jnp.where((col == 245) & (row_r < 7), FAR, tail)
    tail = jnp.where((col == 246) & (row_r == 7), FAR, tail)
    for dw in range(3):
        total = jnp.where(col < 240, pltpu.roll(base, 16 * dw, 1) if dw else base, tail)
        if dw == 0:
            total = jnp.where(col == 243, FAR, total)
        if dw == 2:
            total = jnp.where(col == 244, FAR, total)
        w1_ref[dw * rows : (dw + 1) * rows, :] = total.astype(BF16)
    rows_out[...] = rows_ref[...]


def second_weights(second_ref, bias_ref, head_ref, w2_ref, head_out):
    rows = CH * BAND
    row_r = iota((rows, K2), 0) % BAND
    col = iota((rows, K2), 1)
    col_r = col % 160 // CH
    spread = (iota((rows, CH), 0) // BAND == iota((rows, CH), 1)).astype(F32).astype(BF16)
    f_c = iota((CH, K2), 0)
    f_col = iota((CH, K2), 1)
    second = second_ref[...].reshape(9 * CH, CH)
    by_dw = [
        dot(second, ((f_col // 160 == dw) & (f_col % CH == f_c)).astype(F32).astype(BF16)) for dw in range(3)
    ]
    total = jnp.zeros((rows, K2), F32)
    for a in range(3):
        picked = sum(by_dw[dw][(3 * a + dw) * CH : (3 * a + dw + 1) * CH] for dw in range(3))
        total = total + jnp.where(col_r - row_r == a, dot(spread, picked.astype(BF16)), 0.0)
    total = jnp.where(col >= 480, 0.0, total)
    spread_bias = iota((rows, CH), 0) // BAND == iota((rows, CH), 1)
    for k, piece in enumerate(pieces(bias_ref[...])):
        total = jnp.where(col == 480 + k, column(piece.astype(F32), spread_bias), total)
    w2_ref[...] = total.astype(BF16)
    head_out[...] = jnp.broadcast_to(column(head_ref[...], spread_bias), (rows, LANES))


def weights_kernel(first_ref, first_bias_ref, rows_ref, second_ref, second_bias_ref, head_ref, *outs):
    first_weights(first_ref, first_bias_ref, rows_ref, *outs[:2])
    second_weights(second_ref, second_bias_ref, head_ref, *outs[2:])


def sides_kernel(own_ref, core_ref, chip_ref, sides_ref, *slab_refs):
    odd = lax.axis_index("gx") % 2 == 1
    ends = {}
    for r in range(0, TILE, 16):
        core, chip, own = core_ref[r : r + 16, :], chip_ref[r : r + 16, :], own_ref[r : r + 16, :]
        left = jnp.where(odd, core[:, LANES:], chip[:, LANES:])
        right = jnp.where(odd, chip[:, :LANES], core[:, :LANES])
        sides_ref[r : r + 16, :] = jnp.concatenate([left, right], axis=1)
        ends[r] = jnp.concatenate([left, own, right], axis=1)
    for k, slab_ref in enumerate(slab_refs):
        slab_ref[...] = jnp.where(lax.axis_index("gy") == k, ends[TILE - 16], ends[0])


def shifted(left, own, right):
    wide = jnp.concatenate([left, own, right], axis=1)
    return [wide[:, LANES - 2 + s : LANES - 2 + s + TILE] for s in range(5)]


def ones_rows():
    return jnp.where(iota((16, TILE), 0) < 3, 1.0, 0.0).astype(BF16)


def hidden_band(w1, shifts, last_rows):
    raw = [x.astype(BF16) for x in shifts]
    grid = jnp.concatenate(raw * 3 + [last_rows], axis=0)
    return jnp.maximum(dot(w1, grid), 0.0).astype(BF16)


def restored_band(w2, hidden, ones, head, center):
    deep = dot(w2, jnp.concatenate(hidden + [ones, jnp.zeros((16, TILE), BF16)], axis=0))
    deep = jnp.maximum(deep, 0.0) * jnp.concatenate([head, head], axis=1)
    parts = [deep[o * BAND : (o + 1) * BAND] for o in range(CH)]
    while len(parts) > 1:
        parts = [parts[i] + parts[i + 1] for i in range(0, len(parts), 2)]
    return center + parts[0]


def stage(raw_ref, start, left, own, right):
    for k, x in enumerate(shifted(left, own, right)):
        raw_ref[k, start : start + own.shape[0], :] = x


def stage_own(raw_ref, own_ref, sides_ref):
    for r in range(0, TILE, 16):
        rows = slice(r, r + 16)
        stage(
            raw_ref,
            BAND + r,
            sides_ref[rows, :LANES].astype(F32),
            own_ref[rows, :].astype(F32),
            sides_ref[rows, LANES:].astype(F32),
        )


def first_bands(bands, w1_ref, rows_ref, raw_ref, hid_ref):
    size = BAND * CH
    for j in bands:
        kind = 16 * (1 if j == 0 else 2 if j == BANDS else 0)
        raw = [raw_ref[k, BAND * j : BAND * j + 16, :] for k in range(5)]
        hidden = hidden_band(w1_ref[...], raw, rows_ref[kind : kind + 16, :])
        for dw in range(3):
            hid_ref[dw, j * size : (j + 1) * size, :] = hidden[dw * size : (dw + 1) * size]


def second_bands(bands, w2_ref, head_ref, raw_ref, hid_ref, res_ref):
    ones = ones_rows()
    for b in bands:
        start = (b * BAND + 6) * CH
        hidden = [hid_ref[dw, start : start + 160, :] for dw in range(3)]
        center = raw_ref[2, BAND * (b + 1) : BAND * (b + 2), :]
        res_ref[b * BAND : (b + 1) * BAND, :] = restored_band(w2_ref[...], hidden, ones, head_ref[...], center)


def inner_kernel(
    own_ref,
    sides_ref,
    w1_ref,
    rows_ref,
    w2_ref,
    head_ref,
    out_ref,
    top_ref,
    bottom_ref,
    raw_ref,
    hid_ref,
    res_ref,
):
    size = BAND * CH

    @pl.when(waits())
    def _():
        stage_own(raw_ref, own_ref, sides_ref)
        first_bands(range(1, BANDS), w1_ref, rows_ref, raw_ref, hid_ref)
        top_ref[...] = hid_ref[:, size : 2 * size, :]
        bottom_ref[...] = hid_ref[:, BANDS * size - 2 * CH : BANDS * size, :]
        second_bands(range(1, BANDS - 1), w2_ref, head_ref, raw_ref, hid_ref, res_ref)
        res_ref[0:BAND, :] = jnp.zeros((BAND, TILE), F32)
        res_ref[TILE - BAND :, :] = jnp.zeros((BAND, TILE), F32)
        out_ref[...] = res_ref[...].astype(BF16)


def border(border_refs, place):
    value = jnp.zeros((16, TILE + 2 * LANES), F32)
    for k, ref in enumerate(border_refs):
        value = jnp.where(place == k, ref[...].astype(F32), value)
    return value


def outer_kernel(
    own_ref,
    sides_ref,
    w1_ref,
    rows_ref,
    w2_ref,
    head_ref,
    inner_ref,
    top_ref,
    bottom_ref,
    *refs,
):
    borders, (out_ref, raw_ref, hid_ref, res_ref) = refs[:-4], refs[-4:]
    gy = lax.axis_index("gy")
    size = BAND * CH

    def split(rows):
        return rows[:, :LANES], rows[:, LANES : LANES + TILE], rows[:, LANES + TILE :]

    @pl.when(jnp.logical_not(waits()))
    def _():
        stage(raw_ref, 0, *split(border(borders, gy - 1)[8:16]))
        stage(raw_ref, BAND + TILE, *split(border(borders, gy)[0:8]))
        stage_own(raw_ref, own_ref, sides_ref)
        first_bands(range(BANDS + 1), w1_ref, rows_ref, raw_ref, hid_ref)
        second_bands(range(BANDS), w2_ref, head_ref, raw_ref, hid_ref, res_ref)
        out_ref[...] = res_ref[...].astype(BF16)

    @pl.when(waits())
    def _():
        ones = ones_rows()

        def edge(top):
            near = slice(0, 16) if top else slice(TILE - 16, TILE)
            half = slice(0, 8) if top else slice(8, 16)
            far = split(border(borders, gy - 1)[8:16] if top else border(borders, gy)[0:8])
            own = own_ref[near, :].astype(F32)[half]
            side = sides_ref[near, :].astype(F32)[half]
            parts = (side[:, :LANES], own, side[:, LANES:])
            raw = shifted(*[jnp.concatenate((u, v) if top else (v, u), axis=0) for u, v in zip(far, parts)])
            if top:
                w1 = jnp.concatenate(
                    [w1_ref[(dw + 1) * size - 2 * CH : (dw + 1) * size, :] for dw in range(3)], axis=0
                )
                found = hidden_band(w1, raw, rows_ref[16:32, :])
                hidden = [
                    jnp.concatenate([found[dw * 2 * CH : (dw + 1) * 2 * CH], top_ref[dw]], axis=0)
                    for dw in range(3)
                ]
            else:
                found = hidden_band(w1_ref[...], raw, rows_ref[32:48, :])
                hidden = [
                    jnp.concatenate([bottom_ref[dw], found[dw * size : (dw + 1) * size]], axis=0)
                    for dw in range(3)
                ]
            band = restored_band(w2_ref[...], hidden, ones, head_ref[...], own)
            inner = inner_ref[near, :].astype(F32)
            pair = [band, inner[8:16]] if top else [inner[0:8], band]
            out_ref[near, :] = jnp.concatenate(pair, axis=0).astype(BF16)

        edge(True)
        edge(False)


def transform(image_ref, across_ref, down_ref):
    halves = [
        dot(image_ref[:, q * PATCH : (q + 1) * PATCH], across_ref[...]).astype(BF16) for q in range(2)
    ]
    results = []
    for a in range(2):
        rows = slice(a * PATCH, (a + 1) * PATCH)
        cos_rows = jnp.concatenate([h[rows, :PATCH] for h in halves], axis=1)
        sin_rows = jnp.concatenate([h[rows, PATCH:] for h in halves], axis=1)
        both = dot(down_ref[...], jnp.concatenate([cos_rows, sin_rows], axis=0))
        results.append((both[:PATCH], both[PATCH:]))
    return results


def own_kernel(image_ref, across_ref, down_ref, out_ref):
    for a, (real, imag) in enumerate(transform(image_ref, across_ref, down_ref)):
        rows = slice(a * PATCH, (a + 1) * PATCH)
        out_ref[0, rows, :] = real
        out_ref[1, rows, :] = imag


def cross_kernel(image_ref, across_ref, down_ref, own_ref, out_ref, held_ref, sems):
    copies = []
    for a, (real, imag) in enumerate(transform(image_ref, across_ref, down_ref)):
        rows = slice(a * PATCH, (a + 1) * PATCH)
        own_real, own_imag = own_ref[0, rows, :], own_ref[1, rows, :]
        for part, value in enumerate(
            (own_real * real + own_imag * imag, own_imag * real - own_real * imag)
        ):
            held_ref[part, rows, :] = value
            copies.append(
                pltpu.make_async_copy(held_ref.at[part, rows], out_ref.at[0, part, rows], sems.at[a, part])
            )
            copies[-1].start()
    for copy in copies:
        copy.wait()


def full(shape):
    return pl.BlockSpec(shape, lambda: (0,) * len(shape), memory_space=VMEM)


def call(kernel, name, out_shape, args, scratch=(), flops=0, in_specs=None, out_specs=None, aliases=None):
    return pl.pallas_call(
        kernel,
        name=name,
        out_shape=out_shape,
        in_specs=in_specs or [full(a.shape) for a in args],
        out_specs=out_specs or jax.tree.map(lambda o: full(o.shape), out_shape),
        input_output_aliases=aliases or {},
        scratch_shapes=list(scratch),
        compiler_params=PARAMS,
        cost_estimate=pl.CostEstimate(flops=flops, bytes_accessed=0, transcendentals=0),
    )(*args)


def shaped(*shape, dtype=BF16):
    return jax.ShapeDtypeStruct(shape, dtype)


WEIGHTS = (
    shaped(3 * BAND * CH, K1),
    shaped(48, TILE),
    shaped(CH * BAND, K2),
    shaped(CH * BAND, LANES, dtype=F32),
)
ROOM = (
    pltpu.VMEM((5, TILE + 2 * BAND, TILE), F32),
    pltpu.VMEM((3, (BANDS + 1) * BAND * CH, TILE), BF16),
    pltpu.VMEM((TILE, TILE), F32),
)


def prepare(first, first_bias, second, second_bias, head):
    rows = call(last_rows_kernel, "last_rows", WEIGHTS[1], (), flops=1 << 31)
    given = (first, first_bias, rows, second, second_bias, head)
    return call(weights_kernel, "weights", WEIGHTS, given)


def sides(own, core, chip, borders):
    slab = shaped(16, TILE + 2 * LANES)
    shapes = (shaped(TILE, TILE),) + (slab,) * borders
    return call(sides_kernel, "sides", shapes, (own, core, chip))


def inner(own, side, weights):
    return call(
        inner_kernel,
        "inner_rows",
        (shaped(TILE, TILE), shaped(3, BAND * CH, TILE), shaped(3, 2 * CH, TILE)),
        (own, side, *weights),
        scratch=ROOM,
        flops=3 << 30,
    )


def outer(own, side, weights, inside, borders):
    return call(
        outer_kernel,
        "outer_rows",
        shaped(TILE, TILE),
        (own, side, *weights, *inside, *borders),
        scratch=ROOM,
        flops=3 << 30,
        aliases={6: 0},
    )


def own_spectrum(image, across, down):
    return call(
        own_kernel, "own_spectrum", shaped(2, TILE, TILE, dtype=F32), (image, across, down), flops=1 << 29
    )


def cross_spectrum(image, across, down, own):
    return call(
        cross_kernel,
        "cross_spectrum",
        shaped(1, 2, TILE, TILE, dtype=F32),
        (image, across, down, own),
        scratch=[pltpu.VMEM((2, TILE, TILE), F32), pltpu.SemaphoreType.DMA((2, 2))],
        flops=1 << 29,
        out_specs=pl.BlockSpec(memory_space=pl.ANY),
    )


def from_step(value, axis, step):
    count = lax.axis_size(axis)
    pairs = [(i, i + step) for i in range(count) if 0 <= i + step < count]
    return lax.ppermute(value, axis, pairs)


def swap(value, axis, starts):
    pairs = [(i, i + 1) for i in starts]
    return lax.ppermute(value, axis, pairs + [(j, i) for i, j in pairs])


def on_device(section, first_kernel, first_bias, second_kernel, second_bias, head_weight):
    own = section[0]
    columns, rows = lax.axis_size("gx"), lax.axis_size("gy")
    chip = swap(own, "gx", range(1, columns - 1, 2))
    core = swap(own, "gx", range(0, columns - 1, 2))
    given = (first_kernel, first_bias[None], second_kernel, second_bias[None], head_weight[None])
    weights = prepare(*given)
    side, *slabs = sides(own, core, chip, rows - 1)
    borders = [swap(slab, "gy", [k]) for k, slab in enumerate(slabs)]
    inside = inner(own, side, weights)
    restored = outer(own, side, weights, inside, borders)
    across, down = dft_tables()
    later = from_step(restored, "gz", -1)
    spectrum = own_spectrum(restored, across, down)
    return cross_spectrum(later, across, down, spectrum)


def solution(mesh):
    placed = (P("gz", "gy", "gx"), P(), P(), P(), P(), P())
    return jax.shard_map(
        on_device, mesh=mesh, in_specs=placed, out_specs=P("gz", None, "gy", "gx"), check_vma=False
    )
```

```python
import math

import jax
import jax.numpy as jnp
import numpy as np
from jax import lax
from jax.experimental import pallas as pl
from jax.experimental.pallas import tpu as pltpu
from jax.sharding import PartitionSpec as P

PATCH = 128
TILE = 256
CH = 16
BAND = 8
BANDS = TILE // BAND
LANES = 128
K1 = 256
K2 = 512
FAR = -65536.0

F32 = jnp.float32
BF16 = jnp.bfloat16
VMEM = pltpu.MemorySpace.VMEM
SMEM = pltpu.MemorySpace.SMEM
PARAMS = pltpu.CompilerParams(vmem_limit_bytes=40 * 1024 * 1024)


def dft_tables():
    positions = np.arange(PATCH, dtype=np.int32)
    phase = positions[:, None] * positions[None, :] % PATCH
    angles = phase.astype(np.float32) * np.float32(2.0 * math.pi / PATCH)
    scaling = np.float32(1.0 / math.sqrt(PATCH))
    cosine = (np.cos(angles) * scaling).astype(BF16)
    sine = (np.sin(angles) * scaling).astype(BF16)
    across = np.concatenate([cosine, sine], axis=1)
    down = np.block([[cosine.T, -sine.T], [-sine.T, -cosine.T]]).astype(BF16)
    return across, down


def iota(shape, dim):
    return lax.broadcasted_iota(jnp.int32, shape, dim)


def dot(a, b):
    return lax.dot_general(a, b, (((1,), (0,)), ((), ())), preferred_element_type=F32)


def pieces(values):
    high = values.astype(BF16)
    rest = values - high.astype(F32)
    middle = rest.astype(BF16)
    low = (rest - middle.astype(F32)).astype(BF16)
    return high, middle, low


def column(row, spread):
    return jnp.sum(jnp.where(spread, row, 0.0), axis=1, keepdims=True)


def end_of(axis, last):
    return lax.axis_index(axis) == (lax.axis_size(axis) - 1 if last else 0)


def waits():
    return lax.axis_index("gy") > 0


def last_rows_kernel(rows_out):
    row = iota((16, TILE), 0)
    lane = iota((16, TILE), 1)
    keep = row < 3
    keep = keep | ((row == 3) & (lane == 0) & end_of("gx", False))
    keep = keep | ((row == 4) & (lane == TILE - 1) & end_of("gx", True))
    top = keep | ((row == 5) & end_of("gy", False))
    bottom = keep | ((row == 6) & end_of("gy", True))
    for k, mask in enumerate((keep, top, bottom)):
        rows_out[16 * k : 16 * k + 16, :] = jnp.where(mask, 1.0, 0.0).astype(BF16)


def first_weights(first_ref, bias_ref, rows_ref, w1_ref, rows_out):
    rows = BAND * CH
    row_r = iota((rows, K1), 0) // CH
    col = iota((rows, K1), 1)
    col_i = col % 16
    stacked = jnp.concatenate(pieces(first_ref[...]), axis=0)
    spread = (iota((rows, 48), 0) % CH == iota((rows, 48), 1) % CH).astype(F32).astype(BF16)
    sel_t = iota((9, K1), 0)
    sel_col = iota((9, K1), 1)
    sel_b = sel_col % 80 // 16
    in_grid = (sel_b <= 2) & (sel_col < 240)
    own_piece = iota((48, K1), 0) // CH == iota((48, K1), 1) // 80
    base = jnp.zeros((rows, K1), F32)
    for a in range(3):
        select = (sel_t == 3 * a + sel_b) & in_grid
        picked = dot(stacked, select.astype(F32).astype(BF16))
        picked = jnp.where(own_piece, picked, 0.0).astype(BF16)
        base = base + jnp.where(col_i - row_r == a, dot(spread, picked), 0.0)
    spread_bias = iota((rows, CH), 0) % CH == iota((rows, CH), 1)
    tail = jnp.zeros((rows, K1), F32)
    for k, piece in enumerate(pieces(bias_ref[...])):
        tail = jnp.where(col == 240 + k, column(piece.astype(F32), spread_bias), tail)
    tail = jnp.where((col == 245) & (row_r < 7), FAR, tail)
    tail = jnp.where((col == 246) & (row_r == 7), FAR, tail)
    for dw in range(3):
        total = jnp.where(col < 240, pltpu.roll(base, 16 * dw, 1) if dw else base, tail)
        if dw == 0:
            total = jnp.where(col == 243, FAR, total)
        if dw == 2:
            total = jnp.where(col == 244, FAR, total)
        w1_ref[dw * rows : (dw + 1) * rows, :] = total.astype(BF16)
    rows_out[...] = rows_ref[...]


def second_weights(second_ref, bias_ref, head_ref, w2_ref, head_out):
    rows = CH * BAND
    row_r = iota((rows, K2), 0) % BAND
    col = iota((rows, K2), 1)
    col_r = col % 160 // CH
    spread = (iota((rows, CH), 0) // BAND == iota((rows, CH), 1)).astype(F32).astype(BF16)
    f_c = iota((CH, K2), 0)
    f_col = iota((CH, K2), 1)
    second = second_ref[...].reshape(9 * CH, CH)
    by_dw = [
        dot(second, ((f_col // 160 == dw) & (f_col % CH == f_c)).astype(F32).astype(BF16)) for dw in range(3)
    ]
    total = jnp.zeros((rows, K2), F32)
    for a in range(3):
        picked = sum(by_dw[dw][(3 * a + dw) * CH : (3 * a + dw + 1) * CH] for dw in range(3))
        total = total + jnp.where(col_r - row_r == a, dot(spread, picked.astype(BF16)), 0.0)
    total = jnp.where(col >= 480, 0.0, total)
    spread_bias = iota((rows, CH), 0) // BAND == iota((rows, CH), 1)
    for k, piece in enumerate(pieces(bias_ref[...])):
        total = jnp.where(col == 480 + k, column(piece.astype(F32), spread_bias), total)
    w2_ref[...] = total.astype(BF16)
    head_out[...] = jnp.broadcast_to(column(head_ref[...], spread_bias), (rows, LANES))


def weights_kernel(first_ref, first_bias_ref, rows_ref, second_ref, second_bias_ref, head_ref, *outs):
    first_weights(first_ref, first_bias_ref, rows_ref, *outs[:2])
    second_weights(second_ref, second_bias_ref, head_ref, *outs[2:])


def packed(r0, r1):
    order = [r0[:, LANES : 2 * LANES], r0[:, 2 * LANES : 3 * LANES], r1[:, LANES : 2 * LANES]]
    order += [r1[:, 2 * LANES : 3 * LANES], r0[:, :LANES], r0[:, 3 * LANES :], r1[:, :LANES], r1[:, 3 * LANES :]]
    rows = jnp.concatenate(order, axis=0)
    return jnp.concatenate([rows, rows], axis=0)


def unpacked(block, at):
    def place(r0, r1):
        zeros = [jnp.zeros((n, r0.shape[1]), F32) for n in (at, 6 - at)]
        return jnp.concatenate([x for x in (zeros[0], r0, r1, zeros[1]) if x.shape[0]], axis=0)

    row = [block[k : k + 1] for k in range(8)]
    own = place(jnp.concatenate(row[0:2], axis=1), jnp.concatenate(row[2:4], axis=1))
    return place(row[4], row[6]), own, place(row[5], row[7])


def sides_kernel(own_ref, core_ref, chip_ref, sides_ref, *slab_refs):
    odd = lax.axis_index("gx") % 2 == 1
    ends = {}
    for r in range(0, TILE, 16):
        core, chip = core_ref[r : r + 16, :], chip_ref[r : r + 16, :]
        left = jnp.where(odd, core[:, LANES:], chip[:, LANES:])
        right = jnp.where(odd, chip[:, :LANES], core[:, :LANES])
        sides_ref[r : r + 16, :] = jnp.concatenate([left, right], axis=1)
        if r in (0, TILE - 16):
            wide = jnp.concatenate([left, own_ref[r : r + 16, :], right], axis=1).astype(F32)
            ends[r] = packed(wide[0:1], wide[1:2]) if r == 0 else packed(wide[14:15], wide[15:16])
    for k, slab_ref in enumerate(slab_refs):
        slab_ref[...] = jnp.where(lax.axis_index("gy") == k, ends[TILE - 16], ends[0]).astype(BF16)


def shifted(left, own, right):
    wide = jnp.concatenate([left, own, right], axis=1)
    return [wide[:, LANES - 2 + s : LANES - 2 + s + TILE] for s in range(5)]


def ones_rows():
    return jnp.where(iota((16, TILE), 0) < 3, 1.0, 0.0).astype(BF16)


def hidden_band(w1, shifts, last_rows):
    raw = [x.astype(BF16) for x in shifts]
    grid = jnp.concatenate(raw * 3 + [last_rows], axis=0)
    return jnp.maximum(dot(w1, grid), 0.0).astype(BF16)


def add_up(parts):
    while len(parts) > 1:
        parts = [parts[i] + parts[i + 1] for i in range(0, len(parts), 2)]
    return parts[0]


def restored_band(w2, hidden, ones, head, center):
    deep = dot(w2, jnp.concatenate(hidden + [ones, jnp.zeros((16, TILE), BF16)], axis=0))
    deep = jnp.maximum(deep, 0.0) * jnp.concatenate([head, head], axis=1)
    return center + add_up([deep[o * BAND : (o + 1) * BAND] for o in range(CH)])


def stage(raw_ref, start, left, own, right):
    for k, x in enumerate(shifted(left, own, right)):
        raw_ref[k, start : start + own.shape[0], :] = x


def stage_own(raw_ref, own_ref, sides_ref):
    for r in range(0, TILE, 16):
        rows = slice(r, r + 16)
        stage(
            raw_ref,
            BAND + r,
            sides_ref[rows, :LANES].astype(F32),
            own_ref[rows, :].astype(F32),
            sides_ref[rows, LANES:].astype(F32),
        )


def first_bands(bands, w1_ref, rows_ref, raw_ref, hid_ref):
    size = BAND * CH
    for j in bands:
        kind = 16 * (1 if j == 0 else 2 if j == BANDS else 0)
        raw = [raw_ref[k, BAND * j : BAND * j + 16, :] for k in range(5)]
        hidden = hidden_band(w1_ref[...], raw, rows_ref[kind : kind + 16, :])
        for dw in range(3):
            hid_ref[dw, j * size : (j + 1) * size, :] = hidden[dw * size : (dw + 1) * size]


def second_bands(bands, w2_ref, head_ref, raw_ref, hid_ref, res_ref):
    ones = ones_rows()
    for b in bands:
        start = (b * BAND + 6) * CH
        hidden = [hid_ref[dw, start : start + 160, :] for dw in range(3)]
        center = raw_ref[2, BAND * (b + 1) : BAND * (b + 2), :]
        res_ref[b * BAND : (b + 1) * BAND, :] = restored_band(w2_ref[...], hidden, ones, head_ref[...], center)


def inner_kernel(
    own_ref,
    sides_ref,
    w1_ref,
    rows_ref,
    w2_ref,
    head_ref,
    out_ref,
    top_ref,
    bottom_ref,
    raw_ref,
    hid_ref,
    res_ref,
):
    size = BAND * CH

    @pl.when(waits())
    def _():
        stage_own(raw_ref, own_ref, sides_ref)
        for k in range(5):
            raw_ref[k, BAND + TILE :, :] = jnp.zeros((BAND, TILE), F32)
        first_bands(range(1, BANDS + 1), w1_ref, rows_ref, raw_ref, hid_ref)
        top_ref[...] = hid_ref[:, size : 2 * size, :]
        bottom_ref[...] = hid_ref[:, BANDS * size - 2 * CH : (BANDS + 1) * size - 2 * CH, :]
        second_bands(range(1, BANDS - 1), w2_ref, head_ref, raw_ref, hid_ref, res_ref)
        res_ref[0:BAND, :] = jnp.zeros((BAND, TILE), F32)
        res_ref[TILE - BAND :, :] = jnp.zeros((BAND, TILE), F32)
        out_ref[...] = res_ref[...].astype(BF16)


def border(border_refs, place):
    value = jnp.zeros((16, LANES), F32)
    for k, ref in enumerate(border_refs):
        value = jnp.where(place == k, ref[...].astype(F32), value)
    return value


def outer_kernel(
    own_ref,
    sides_ref,
    w1_ref,
    rows_ref,
    w2_ref,
    head_ref,
    inner_ref,
    top_ref,
    bottom_ref,
    *refs,
):
    borders, (out_ref, raw_ref, hid_ref, res_ref) = refs[:-4], refs[-4:]
    gy = lax.axis_index("gy")
    size = BAND * CH

    def above():
        return unpacked(border(borders, gy - 1), 6)

    def below():
        return unpacked(border(borders, gy), 0)

    @pl.when(jnp.logical_not(waits()))
    def _():
        stage(raw_ref, 0, *above())
        stage(raw_ref, BAND + TILE, *below())
        stage_own(raw_ref, own_ref, sides_ref)
        first_bands(range(BANDS + 1), w1_ref, rows_ref, raw_ref, hid_ref)
        second_bands(range(BANDS), w2_ref, head_ref, raw_ref, hid_ref, res_ref)
        out_ref[...] = res_ref[...].astype(BF16)

    @pl.when(waits())
    def _():
        first, last = slice(0, 16), slice(TILE - 16, TILE)
        own = own_ref[first, :].astype(F32)[0:8], own_ref[last, :].astype(F32)[8:16]
        side = sides_ref[first, :].astype(F32)[0:8], sides_ref[last, :].astype(F32)[8:16]
        near = [(s[:, :LANES], o, s[:, LANES:]) for s, o in zip(side, own)]
        top = shifted(*[jnp.concatenate(pair, axis=0) for pair in zip(above(), near[0])])
        bottom = shifted(*[jnp.concatenate(pair, axis=0) for pair in zip(near[1], below())])
        grids = []
        for raw, rows in ((top, rows_ref[16:32, :]), (bottom, rows_ref[32:48, :])):
            grids.append(jnp.concatenate([x.astype(BF16) for x in raw] * 3 + [rows], axis=0))
        w1 = jnp.concatenate([w1_ref[(dw + 1) * size - 2 * CH : (dw + 1) * size, :] for dw in range(3)], axis=0)
        found = jnp.maximum(dot(w1, jnp.concatenate(grids, axis=1)), 0.0).astype(BF16)
        hidden = []
        for dw in range(3):
            two = found[dw * 2 * CH : (dw + 1) * 2 * CH]
            upper = jnp.concatenate([two[:, :TILE], top_ref[dw]], axis=0)
            lower = jnp.concatenate([bottom_ref[dw], two[:, TILE:]], axis=0)
            hidden.append(jnp.concatenate([upper, lower], axis=1))
        tail = jnp.concatenate([ones_rows(), jnp.zeros((16, TILE), BF16)], axis=0)
        hidden.append(jnp.concatenate([tail, tail], axis=1))
        deep = jnp.maximum(dot(w2_ref[...], jnp.concatenate(hidden, axis=0)), 0.0)
        deep = deep * jnp.concatenate([head_ref[...]] * 4, axis=1)
        total = add_up([deep[o * BAND : (o + 1) * BAND] for o in range(CH)])
        upper = own[0] + total[:, :TILE]
        lower = own[1] + total[:, TILE:]
        out_ref[first, :] = jnp.concatenate([upper, inner_ref[first, :].astype(F32)[8:16]], axis=0).astype(BF16)
        out_ref[last, :] = jnp.concatenate([inner_ref[last, :].astype(F32)[0:8], lower], axis=0).astype(BF16)


def transform(image_ref, across_ref, down_ref):
    halves = [
        dot(image_ref[:, q * PATCH : (q + 1) * PATCH], across_ref[...]).astype(BF16) for q in range(2)
    ]
    results = []
    for a in range(2):
        rows = slice(a * PATCH, (a + 1) * PATCH)
        cos_rows = jnp.concatenate([h[rows, :PATCH] for h in halves], axis=1)
        sin_rows = jnp.concatenate([h[rows, PATCH:] for h in halves], axis=1)
        both = dot(down_ref[...], jnp.concatenate([cos_rows, sin_rows], axis=0))
        results.append((both[:PATCH], both[PATCH:]))
    return results


def own_kernel(image_ref, across_ref, down_ref, out_ref):
    for a, (real, imag) in enumerate(transform(image_ref, across_ref, down_ref)):
        rows = slice(a * PATCH, (a + 1) * PATCH)
        out_ref[0, rows, :] = real
        out_ref[1, rows, :] = imag


def cross_kernel(image_ref, across_ref, down_ref, own_ref, out_ref, held_ref, sems):
    copies = []
    for a, (real, imag) in enumerate(transform(image_ref, across_ref, down_ref)):
        rows = slice(a * PATCH, (a + 1) * PATCH)
        own_real, own_imag = own_ref[0, rows, :], own_ref[1, rows, :]
        for part, value in enumerate(
            (own_real * real + own_imag * imag, own_imag * real - own_real * imag)
        ):
            held_ref[part, rows, :] = value
            copies.append(
                pltpu.make_async_copy(held_ref.at[part, rows], out_ref.at[0, part, rows], sems.at[a, part])
            )
            copies[-1].start()
    for copy in copies:
        copy.wait()


def full(shape):
    return pl.BlockSpec(shape, lambda: (0,) * len(shape), memory_space=VMEM)


def call(kernel, name, out_shape, args, scratch=(), flops=0, in_specs=None, out_specs=None, aliases=None):
    return pl.pallas_call(
        kernel,
        name=name,
        out_shape=out_shape,
        in_specs=in_specs or [full(a.shape) for a in args],
        out_specs=out_specs or jax.tree.map(lambda o: full(o.shape), out_shape),
        input_output_aliases=aliases or {},
        scratch_shapes=list(scratch),
        compiler_params=PARAMS,
        cost_estimate=pl.CostEstimate(flops=flops, bytes_accessed=0, transcendentals=0),
    )(*args)


def shaped(*shape, dtype=BF16):
    return jax.ShapeDtypeStruct(shape, dtype)


WEIGHTS = (
    shaped(3 * BAND * CH, K1),
    shaped(48, TILE),
    shaped(CH * BAND, K2),
    shaped(CH * BAND, LANES, dtype=F32),
)
ROOM = (
    pltpu.VMEM((5, TILE + 2 * BAND, TILE), F32),
    pltpu.VMEM((3, (BANDS + 1) * BAND * CH, TILE), BF16),
    pltpu.VMEM((TILE, TILE), F32),
)


def prepare(first, first_bias, second, second_bias, head):
    rows = call(last_rows_kernel, "last_rows", WEIGHTS[1], (), flops=1 << 31)
    given = (first, first_bias, rows, second, second_bias, head)
    return call(weights_kernel, "weights", WEIGHTS, given)


def sides(own, core, chip, borders):
    slab = shaped(16, LANES)
    shapes = (shaped(TILE, TILE),) + (slab,) * borders
    return call(sides_kernel, "sides", shapes, (own, core, chip))


def inner(own, side, weights):
    return call(
        inner_kernel,
        "inner_rows",
        (shaped(TILE, TILE), shaped(3, BAND * CH, TILE), shaped(3, BAND * CH, TILE)),
        (own, side, *weights),
        scratch=ROOM,
        flops=3 << 30,
    )


def outer(own, side, weights, inside, borders):
    return call(
        outer_kernel,
        "outer_rows",
        shaped(TILE, TILE),
        (own, side, *weights, *inside, *borders),
        scratch=ROOM,
        flops=3 << 30,
        aliases={6: 0},
    )


def own_spectrum(image, across, down):
    return call(
        own_kernel, "own_spectrum", shaped(2, TILE, TILE, dtype=F32), (image, across, down), flops=1 << 29
    )


def cross_spectrum(image, across, down, own):
    return call(
        cross_kernel,
        "cross_spectrum",
        shaped(1, 2, TILE, TILE, dtype=F32),
        (image, across, down, own),
        scratch=[pltpu.VMEM((2, TILE, TILE), F32), pltpu.SemaphoreType.DMA((2, 2))],
        flops=1 << 29,
        out_specs=pl.BlockSpec(memory_space=pl.ANY),
    )


def from_step(value, axis, step):
    count = lax.axis_size(axis)
    pairs = [(i, i + step) for i in range(count) if 0 <= i + step < count]
    return lax.ppermute(value, axis, pairs)


def swap(value, axis, starts):
    pairs = [(i, i + 1) for i in starts]
    return lax.ppermute(value, axis, pairs + [(j, i) for i, j in pairs])


def on_device(section, first_kernel, first_bias, second_kernel, second_bias, head_weight):
    own = section[0]
    columns, rows = lax.axis_size("gx"), lax.axis_size("gy")
    chip = swap(own, "gx", range(1, columns - 1, 2))
    core = swap(own, "gx", range(0, columns - 1, 2))
    given = (first_kernel, first_bias[None], second_kernel, second_bias[None], head_weight[None])
    weights = prepare(*given)
    side, *slabs = sides(own, core, chip, rows - 1)
    borders = [swap(slab, "gy", [k]) for k, slab in enumerate(slabs)]
    inside = inner(own, side, weights)
    restored = outer(own, side, weights, inside, borders)
    across, down = dft_tables()
    later = from_step(restored, "gz", -1)
    spectrum = own_spectrum(restored, across, down)
    return cross_spectrum(later, across, down, spectrum)


def solution(mesh):
    placed = (P("gz", "gy", "gx"), P(), P(), P(), P(), P())
    return jax.shard_map(
        on_device, mesh=mesh, in_specs=placed, out_specs=P("gz", None, "gy", "gx"), check_vma=False
    )
```

```python
import math

import jax
import jax.numpy as jnp
import numpy as np
from jax import lax
from jax.experimental import pallas as pl
from jax.experimental.pallas import tpu as pltpu
from jax.sharding import PartitionSpec as P

PATCH = 128
TILE = 256
CH = 16
BAND = 8
BANDS = TILE // BAND
LANES = 128
K1 = 160
RING = TILE + LANES
K2 = 512
FAR = -65536.0

F32 = jnp.float32
BF16 = jnp.bfloat16
VMEM = pltpu.MemorySpace.VMEM
SMEM = pltpu.MemorySpace.SMEM
PARAMS = pltpu.CompilerParams(vmem_limit_bytes=40 * 1024 * 1024)


def dft_tables():
    positions = np.arange(PATCH, dtype=np.int32)
    phase = positions[:, None] * positions[None, :] % PATCH
    angles = phase.astype(np.float32) * np.float32(2.0 * math.pi / PATCH)
    scaling = np.float32(1.0 / math.sqrt(PATCH))
    cosine = (np.cos(angles) * scaling).astype(BF16)
    sine = (np.sin(angles) * scaling).astype(BF16)
    across = np.concatenate([cosine, sine], axis=1)
    down = np.block([[cosine.T, -sine.T], [-sine.T, -cosine.T]]).astype(BF16)
    return across, down


def iota(shape, dim):
    return lax.broadcasted_iota(jnp.int32, shape, dim)


def dot(a, b):
    return lax.dot_general(a, b, (((1,), (0,)), ((), ())), preferred_element_type=F32)


def pieces(values):
    high = values.astype(BF16)
    rest = values - high.astype(F32)
    middle = rest.astype(BF16)
    low = (rest - middle.astype(F32)).astype(BF16)
    return high, middle, low


def column(row, spread):
    return jnp.sum(jnp.where(spread, row, 0.0), axis=1, keepdims=True)


def end_of(axis, last):
    return lax.axis_index(axis) == (lax.axis_size(axis) - 1 if last else 0)


def waits():
    return lax.axis_index("gy") > 0


def last_rows_kernel(rows_out):
    row = iota((16, RING), 0)
    lane = iota((16, RING), 1)
    keep = row < 3
    keep = keep | ((row == 3) & (lane == RING - 1) & end_of("gx", False))
    keep = keep | ((row == 3) & (lane == TILE) & end_of("gx", True))
    top = keep | ((row == 5) & end_of("gy", False))
    bottom = keep | ((row == 6) & end_of("gy", True))
    for k, mask in enumerate((keep, top, bottom)):
        rows_out[16 * k : 16 * k + 16, :] = jnp.where(mask, 1.0, 0.0).astype(BF16)


def first_weights(first_ref, bias_ref, rows_ref, w1_ref, rows_out):
    rows = BAND * CH
    row_r = iota((rows, K1), 0) // CH
    col = iota((rows, K1), 1)
    col_i = col % 16
    stacked = jnp.concatenate(pieces(first_ref[...]), axis=0)
    spread = (iota((rows, 48), 0) % CH == iota((rows, 48), 1) % CH).astype(F32).astype(BF16)
    sel_t = iota((9, K1), 0)
    sel_col = iota((9, K1), 1)
    sel_b = sel_col % 48 // 16
    own_piece = iota((48, K1), 0) // CH == iota((48, K1), 1) // 48
    total = jnp.zeros((rows, K1), F32)
    for a in range(3):
        select = (sel_t == 3 * a + sel_b) & (sel_col < 144)
        picked = dot(stacked, select.astype(F32).astype(BF16))
        picked = jnp.where(own_piece, picked, 0.0).astype(BF16)
        total = total + jnp.where(col_i - row_r == a, dot(spread, picked), 0.0)
    spread_bias = iota((rows, CH), 0) % CH == iota((rows, CH), 1)
    total = jnp.where(col < 144, total, 0.0)
    for k, piece in enumerate(pieces(bias_ref[...])):
        total = jnp.where(col == 144 + k, column(piece.astype(F32), spread_bias), total)
    total = jnp.where(col == 147, FAR, total)
    total = jnp.where((col == 149) & (row_r < 7), FAR, total)
    total = jnp.where((col == 150) & (row_r == 7), FAR, total)
    w1_ref[...] = total.astype(BF16)
    rows_out[...] = rows_ref[...]


def second_weights(second_ref, bias_ref, head_ref, w2_ref, head_out):
    rows = CH * BAND
    row_r = iota((rows, K2), 0) % BAND
    col = iota((rows, K2), 1)
    col_r = col % 160 // CH
    spread = (iota((rows, CH), 0) // BAND == iota((rows, CH), 1)).astype(F32).astype(BF16)
    f_c = iota((CH, K2), 0)
    f_col = iota((CH, K2), 1)
    second = second_ref[...].reshape(9 * CH, CH)
    by_dw = [
        dot(second, ((f_col // 160 == dw) & (f_col % CH == f_c)).astype(F32).astype(BF16)) for dw in range(3)
    ]
    total = jnp.zeros((rows, K2), F32)
    for a in range(3):
        picked = sum(by_dw[dw][(3 * a + dw) * CH : (3 * a + dw + 1) * CH] for dw in range(3))
        total = total + jnp.where(col_r - row_r == a, dot(spread, picked.astype(BF16)), 0.0)
    total = jnp.where(col >= 480, 0.0, total)
    spread_bias = iota((rows, CH), 0) // BAND == iota((rows, CH), 1)
    for k, piece in enumerate(pieces(bias_ref[...])):
        total = jnp.where(col == 480 + k, column(piece.astype(F32), spread_bias), total)
    w2_ref[...] = total.astype(BF16)
    head_out[...] = jnp.broadcast_to(column(head_ref[...], spread_bias), (rows, LANES))


def weights_kernel(first_ref, first_bias_ref, rows_ref, second_ref, second_bias_ref, head_ref, *outs):
    first_weights(first_ref, first_bias_ref, rows_ref, *outs[:2])
    second_weights(second_ref, second_bias_ref, head_ref, *outs[2:])


def packed(r0, r1):
    rows = [r[:, k * LANES : (k + 1) * LANES] for r in (r0, r1) for k in range(3)]
    rows = jnp.concatenate(rows + [jnp.zeros((2, LANES), F32)], axis=0)
    return jnp.concatenate([rows, rows], axis=0)


def unpacked(block, at):
    r0, r1 = (jnp.concatenate([block[k + j : k + j + 1] for j in range(3)], axis=1) for k in (0, 3))
    zeros = [jnp.zeros((n, RING), F32) for n in (at, 6 - at)]
    return jnp.concatenate([x for x in (zeros[0], r0, r1, zeros[1]) if x.shape[0]], axis=0)


def sides_kernel(own_ref, core_ref, chip_ref, sides_ref, *slab_refs):
    odd = lax.axis_index("gx") % 2 == 1
    first = iota((16, LANES), 1) < LANES // 2
    ends = {}
    for r in range(0, TILE, 16):
        core, chip = core_ref[r : r + 16, :].astype(F32), chip_ref[r : r + 16, :].astype(F32)
        left = jnp.where(odd, core[:, LANES:], chip[:, LANES:])
        right = jnp.where(odd, chip[:, :LANES], core[:, :LANES])
        side = jnp.where(first, right, left)
        sides_ref[r : r + 16, :] = side.astype(BF16)
        if r in (0, TILE - 16):
            ring = jnp.concatenate([own_ref[r : r + 16, :].astype(F32), side], axis=1)
            ends[r] = packed(ring[0:1], ring[1:2]) if r == 0 else packed(ring[14:15], ring[15:16])
    for k, slab_ref in enumerate(slab_refs):
        slab_ref[...] = jnp.where(lax.axis_index("gy") == k, ends[TILE - 16], ends[0]).astype(BF16)


def around(ring):
    return [pltpu.roll(ring, 1, 1), ring, pltpu.roll(ring, RING - 1, 1)]


def ones_rows():
    return jnp.where(iota((16, TILE), 0) < 3, 1.0, 0.0).astype(BF16)


def add_up(parts):
    while len(parts) > 1:
        parts = [parts[i] + parts[i + 1] for i in range(0, len(parts), 2)]
    return parts[0]


def stage(raw_ref, start, ring):
    for k, x in enumerate(around(ring)):
        raw_ref[k, start : start + ring.shape[0], :] = x


def stage_own(raw_ref, own_ref, sides_ref):
    for r in range(0, TILE, 16):
        rows = slice(r, r + 16)
        ring = jnp.concatenate([own_ref[rows, :].astype(F32), sides_ref[rows, :].astype(F32)], axis=1)
        stage(raw_ref, BAND + r, ring)


def first_bands(bands, w1_ref, rows_ref, raw_ref, hid_ref):
    size = BAND * CH

    def grid(j):
        kind = 16 * (1 if j == 0 else 2 if j == BANDS else 0)
        raw = [raw_ref[k, BAND * j : BAND * j + 16, :].astype(BF16) for k in range(3)]
        return jnp.concatenate(raw * 3 + [rows_ref[kind : kind + 16, :]], axis=0)

    def keep(j, ring):
        for dw, x in enumerate(around(ring)):
            hid_ref[dw, j * size : (j + 1) * size, :] = x[:, :TILE]

    bands = list(bands)
    while bands:
        now, bands = bands[:2], bands[2:]
        grids = [grid(j) for j in now]
        if len(now) == 2:
            grids[1] = jnp.concatenate([grids[1][:, TILE:], grids[1][:, :TILE]], axis=1)
        found = jnp.maximum(dot(w1_ref[...], jnp.concatenate(grids, axis=1)), 0.0).astype(BF16)
        keep(now[0], found[:, :RING])
        if len(now) == 2:
            keep(now[1], jnp.concatenate([found[:, RING + LANES :], found[:, RING : RING + LANES]], axis=1))


def second_bands(bands, w2_ref, head_ref, raw_ref, hid_ref, res_ref):
    tail = jnp.concatenate([ones_rows(), jnp.zeros((16, TILE), BF16)], axis=0)
    bands = list(bands)
    while bands:
        now, bands = bands[:2], bands[2:]
        grids = []
        for b in now:
            start = (b * BAND + 6) * CH
            grids.append(jnp.concatenate([hid_ref[dw, start : start + 160, :] for dw in range(3)] + [tail], axis=0))
        deep = jnp.maximum(dot(w2_ref[...], jnp.concatenate(grids, axis=1)), 0.0)
        deep = deep * jnp.concatenate([head_ref[...]] * (2 * len(now)), axis=1)
        total = add_up([deep[o * BAND : (o + 1) * BAND] for o in range(CH)])
        for n, b in enumerate(now):
            center = raw_ref[1, BAND * (b + 1) : BAND * (b + 2), :TILE]
            res_ref[b * BAND : (b + 1) * BAND, :] = center + total[:, n * TILE : (n + 1) * TILE]


def inner_kernel(
    own_ref,
    sides_ref,
    w1_ref,
    rows_ref,
    w2_ref,
    head_ref,
    out_ref,
    top_ref,
    bottom_ref,
    raw_ref,
    hid_ref,
    res_ref,
):
    size = BAND * CH

    @pl.when(waits())
    def _():
        stage_own(raw_ref, own_ref, sides_ref)
        for k in range(3):
            raw_ref[k, BAND + TILE :, :] = jnp.zeros((BAND, RING), F32)
        first_bands(range(1, BANDS + 1), w1_ref, rows_ref, raw_ref, hid_ref)
        top_ref[...] = hid_ref[:, size : 2 * size, :]
        bottom_ref[...] = hid_ref[:, BANDS * size - 2 * CH : (BANDS + 1) * size - 2 * CH, :]
        second_bands(range(1, BANDS - 1), w2_ref, head_ref, raw_ref, hid_ref, res_ref)
        res_ref[0:BAND, :] = jnp.zeros((BAND, TILE), F32)
        res_ref[TILE - BAND :, :] = jnp.zeros((BAND, TILE), F32)
        out_ref[...] = res_ref[...].astype(BF16)


def border(border_refs, place):
    value = jnp.zeros((16, LANES), F32)
    for k, ref in enumerate(border_refs):
        value = jnp.where(place == k, ref[...].astype(F32), value)
    return value


def outer_kernel(
    own_ref,
    sides_ref,
    w1_ref,
    rows_ref,
    w2_ref,
    head_ref,
    inner_ref,
    top_ref,
    bottom_ref,
    *refs,
):
    borders, (out_ref, raw_ref, hid_ref, res_ref) = refs[:-4], refs[-4:]
    gy = lax.axis_index("gy")
    size = BAND * CH

    def above():
        return unpacked(border(borders, gy - 1), 6)

    def below():
        return unpacked(border(borders, gy), 0)

    @pl.when(jnp.logical_not(waits()))
    def _():
        stage(raw_ref, 0, above())
        stage(raw_ref, BAND + TILE, below())
        stage_own(raw_ref, own_ref, sides_ref)
        first_bands(range(BANDS + 1), w1_ref, rows_ref, raw_ref, hid_ref)
        second_bands(range(BANDS), w2_ref, head_ref, raw_ref, hid_ref, res_ref)
        out_ref[...] = res_ref[...].astype(BF16)

    @pl.when(waits())
    def _():
        first, last = slice(0, 16), slice(TILE - 16, TILE)
        own = own_ref[first, :].astype(F32)[0:8], own_ref[last, :].astype(F32)[8:16]
        side = sides_ref[first, :].astype(F32)[0:8], sides_ref[last, :].astype(F32)[8:16]
        near = [jnp.concatenate(pair, axis=1) for pair in zip(own, side)]
        grids = []
        for ring, rows in (
            (jnp.concatenate([above(), near[0]], axis=0), rows_ref[16:32, :]),
            (jnp.concatenate([near[1], below()], axis=0), rows_ref[32:48, :]),
        ):
            grids.append(jnp.concatenate([x.astype(BF16) for x in around(ring)] * 3 + [rows], axis=0))
        found = jnp.maximum(dot(w1_ref[size - 2 * CH :, :], jnp.concatenate(grids, axis=1)), 0.0)
        found = [[x[:, :TILE].astype(BF16) for x in around(found[:, n * RING : (n + 1) * RING])] for n in range(2)]
        hidden = []
        for dw in range(3):
            upper = jnp.concatenate([found[0][dw], top_ref[dw]], axis=0)
            lower = jnp.concatenate([bottom_ref[dw], found[1][dw]], axis=0)
            hidden.append(jnp.concatenate([upper, lower], axis=1))
        tail = jnp.concatenate([ones_rows(), jnp.zeros((16, TILE), BF16)], axis=0)
        hidden.append(jnp.concatenate([tail, tail], axis=1))
        deep = jnp.maximum(dot(w2_ref[...], jnp.concatenate(hidden, axis=0)), 0.0)
        deep = deep * jnp.concatenate([head_ref[...]] * 4, axis=1)
        total = add_up([deep[o * BAND : (o + 1) * BAND] for o in range(CH)])
        upper = own[0] + total[:, :TILE]
        lower = own[1] + total[:, TILE:]
        out_ref[first, :] = jnp.concatenate([upper, inner_ref[first, :].astype(F32)[8:16]], axis=0).astype(BF16)
        out_ref[last, :] = jnp.concatenate([inner_ref[last, :].astype(F32)[0:8], lower], axis=0).astype(BF16)


def transform(image_ref, across_ref, down_ref):
    halves = [
        dot(image_ref[:, q * PATCH : (q + 1) * PATCH], across_ref[...]).astype(BF16) for q in range(2)
    ]
    results = []
    for a in range(2):
        rows = slice(a * PATCH, (a + 1) * PATCH)
        cos_rows = jnp.concatenate([h[rows, :PATCH] for h in halves], axis=1)
        sin_rows = jnp.concatenate([h[rows, PATCH:] for h in halves], axis=1)
        both = dot(down_ref[...], jnp.concatenate([cos_rows, sin_rows], axis=0))
        results.append((both[:PATCH], both[PATCH:]))
    return results


def own_kernel(image_ref, across_ref, down_ref, out_ref):
    for a, (real, imag) in enumerate(transform(image_ref, across_ref, down_ref)):
        rows = slice(a * PATCH, (a + 1) * PATCH)
        out_ref[0, rows, :] = real
        out_ref[1, rows, :] = imag


def cross_kernel(image_ref, across_ref, down_ref, own_ref, out_ref, held_ref, sems):
    copies = []
    for a, (real, imag) in enumerate(transform(image_ref, across_ref, down_ref)):
        rows = slice(a * PATCH, (a + 1) * PATCH)
        own_real, own_imag = own_ref[0, rows, :], own_ref[1, rows, :]
        for part, value in enumerate(
            (own_real * real + own_imag * imag, own_imag * real - own_real * imag)
        ):
            held_ref[part, rows, :] = value
            copies.append(
                pltpu.make_async_copy(held_ref.at[part, rows], out_ref.at[0, part, rows], sems.at[a, part])
            )
            copies[-1].start()
    for copy in copies:
        copy.wait()


def full(shape):
    return pl.BlockSpec(shape, lambda: (0,) * len(shape), memory_space=VMEM)


def call(kernel, name, out_shape, args, scratch=(), flops=0, in_specs=None, out_specs=None, aliases=None):
    return pl.pallas_call(
        kernel,
        name=name,
        out_shape=out_shape,
        in_specs=in_specs or [full(a.shape) for a in args],
        out_specs=out_specs or jax.tree.map(lambda o: full(o.shape), out_shape),
        input_output_aliases=aliases or {},
        scratch_shapes=list(scratch),
        compiler_params=PARAMS,
        cost_estimate=pl.CostEstimate(flops=flops, bytes_accessed=0, transcendentals=0),
    )(*args)


def shaped(*shape, dtype=BF16):
    return jax.ShapeDtypeStruct(shape, dtype)


WEIGHTS = (
    shaped(BAND * CH, K1),
    shaped(48, RING),
    shaped(CH * BAND, K2),
    shaped(CH * BAND, LANES, dtype=F32),
)
ROOM = (
    pltpu.VMEM((3, TILE + 2 * BAND, RING), F32),
    pltpu.VMEM((3, (BANDS + 1) * BAND * CH, TILE), BF16),
    pltpu.VMEM((TILE, TILE), F32),
)


def prepare(first, first_bias, second, second_bias, head):
    rows = call(last_rows_kernel, "last_rows", WEIGHTS[1], (), flops=1 << 31)
    given = (first, first_bias, rows, second, second_bias, head)
    return call(weights_kernel, "weights", WEIGHTS, given)


def sides(own, core, chip, borders):
    slab = shaped(16, LANES)
    shapes = (shaped(TILE, LANES),) + (slab,) * borders
    return call(sides_kernel, "sides", shapes, (own, core, chip))


def inner(own, side, weights):
    return call(
        inner_kernel,
        "inner_rows",
        (shaped(TILE, TILE), shaped(3, BAND * CH, TILE), shaped(3, BAND * CH, TILE)),
        (own, side, *weights),
        scratch=ROOM,
        flops=3 << 30,
    )


def outer(own, side, weights, inside, borders):
    return call(
        outer_kernel,
        "outer_rows",
        shaped(TILE, TILE),
        (own, side, *weights, *inside, *borders),
        scratch=ROOM,
        flops=3 << 30,
        aliases={6: 0},
    )


def own_spectrum(image, across, down):
    return call(
        own_kernel, "own_spectrum", shaped(2, TILE, TILE, dtype=F32), (image, across, down), flops=1 << 29
    )


def cross_spectrum(image, across, down, own):
    return call(
        cross_kernel,
        "cross_spectrum",
        shaped(1, 2, TILE, TILE, dtype=F32),
        (image, across, down, own),
        scratch=[pltpu.VMEM((2, TILE, TILE), F32), pltpu.SemaphoreType.DMA((2, 2))],
        flops=1 << 29,
        out_specs=pl.BlockSpec(memory_space=pl.ANY),
    )


def from_step(value, axis, step):
    count = lax.axis_size(axis)
    pairs = [(i, i + step) for i in range(count) if 0 <= i + step < count]
    return lax.ppermute(value, axis, pairs)


def swap(value, axis, starts):
    pairs = [(i, i + 1) for i in starts]
    return lax.ppermute(value, axis, pairs + [(j, i) for i, j in pairs])


def on_device(section, first_kernel, first_bias, second_kernel, second_bias, head_weight):
    own = section[0]
    columns, rows = lax.axis_size("gx"), lax.axis_size("gy")
    chip = swap(own, "gx", range(1, columns - 1, 2))
    core = swap(own, "gx", range(0, columns - 1, 2))
    given = (first_kernel, first_bias[None], second_kernel, second_bias[None], head_weight[None])
    weights = prepare(*given)
    side, *slabs = sides(own, core, chip, rows - 1)
    borders = [swap(slab, "gy", [k]) for k, slab in enumerate(slabs)]
    inside = inner(own, side, weights)
    restored = outer(own, side, weights, inside, borders)
    across, down = dft_tables()
    later = from_step(restored, "gz", -1)
    spectrum = own_spectrum(restored, across, down)
    return cross_spectrum(later, across, down, spectrum)


def solution(mesh):
    placed = (P("gz", "gy", "gx"), P(), P(), P(), P(), P())
    return jax.shard_map(
        on_device, mesh=mesh, in_specs=placed, out_specs=P("gz", None, "gy", "gx"), check_vma=False
    )
```

```python
import math

import jax
import jax.numpy as jnp
import numpy as np
from jax import lax
from jax.experimental import pallas as pl
from jax.experimental.pallas import tpu as pltpu
from jax.sharding import PartitionSpec as P

PATCH = 128
TILE = 256
CH = 16
BAND = 8
BANDS = TILE // BAND
LANES = 128
K1 = 160
RING = TILE + LANES
K2 = 512
FAR = -65536.0

F32 = jnp.float32
BF16 = jnp.bfloat16
VMEM = pltpu.MemorySpace.VMEM
SMEM = pltpu.MemorySpace.SMEM
PARAMS = pltpu.CompilerParams(vmem_limit_bytes=40 * 1024 * 1024)


def dft_tables():
    positions = np.arange(PATCH, dtype=np.int32)
    phase = positions[:, None] * positions[None, :] % PATCH
    angles = phase.astype(np.float32) * np.float32(2.0 * math.pi / PATCH)
    scaling = np.float32(1.0 / math.sqrt(PATCH))
    cosine = (np.cos(angles) * scaling).astype(BF16)
    sine = (np.sin(angles) * scaling).astype(BF16)
    across = np.concatenate([cosine, sine], axis=1)
    down = np.block([[cosine.T, -sine.T], [-sine.T, -cosine.T]]).astype(BF16)
    return across, down


def iota(shape, dim):
    return lax.broadcasted_iota(jnp.int32, shape, dim)


def dot(a, b):
    return lax.dot_general(a, b, (((1,), (0,)), ((), ())), preferred_element_type=F32)


def pieces(values):
    high = values.astype(BF16)
    rest = values - high.astype(F32)
    middle = rest.astype(BF16)
    low = (rest - middle.astype(F32)).astype(BF16)
    return high, middle, low


def column(row, spread):
    return jnp.sum(jnp.where(spread, row, 0.0), axis=1, keepdims=True)


def end_of(axis, last):
    return lax.axis_index(axis) == (lax.axis_size(axis) - 1 if last else 0)


def deep_half():
    return lax.axis_index("gz") >= lax.axis_size("gz") // 2


def early():
    return (lax.axis_index("gy") == 0) & deep_half()


def waits():
    return (lax.axis_index("gy") > 0) | deep_half()


def last_rows_kernel(rows_out):
    row = iota((16, RING), 0)
    lane = iota((16, RING), 1)
    keep = row < 3
    keep = keep | ((row == 3) & (lane == RING - 1) & end_of("gx", False))
    keep = keep | ((row == 3) & (lane == TILE) & end_of("gx", True))
    top = keep | ((row == 5) & end_of("gy", False))
    bottom = keep | ((row == 6) & end_of("gy", True))
    for k, mask in enumerate((keep, top, bottom)):
        rows_out[16 * k : 16 * k + 16, :] = jnp.where(mask, 1.0, 0.0).astype(BF16)


def first_weights(first_ref, bias_ref, rows_ref, w1_ref, rows_out):
    rows = BAND * CH
    row_r = iota((rows, K1), 0) // CH
    col = iota((rows, K1), 1)
    col_i = col % 16
    stacked = jnp.concatenate(pieces(first_ref[...]), axis=0)
    spread = (iota((rows, 48), 0) % CH == iota((rows, 48), 1) % CH).astype(F32).astype(BF16)
    sel_t = iota((9, K1), 0)
    sel_col = iota((9, K1), 1)
    sel_b = sel_col % 48 // 16
    own_piece = iota((48, K1), 0) // CH == iota((48, K1), 1) // 48
    total = jnp.zeros((rows, K1), F32)
    for a in range(3):
        select = (sel_t == 3 * a + sel_b) & (sel_col < 144)
        picked = dot(stacked, select.astype(F32).astype(BF16))
        picked = jnp.where(own_piece, picked, 0.0).astype(BF16)
        total = total + jnp.where(col_i - row_r == a, dot(spread, picked), 0.0)
    spread_bias = iota((rows, CH), 0) % CH == iota((rows, CH), 1)
    total = jnp.where(col < 144, total, 0.0)
    for k, piece in enumerate(pieces(bias_ref[...])):
        total = jnp.where(col == 144 + k, column(piece.astype(F32), spread_bias), total)
    total = jnp.where(col == 147, FAR, total)
    total = jnp.where((col == 149) & (row_r < 7), FAR, total)
    total = jnp.where((col == 150) & (row_r == 7), FAR, total)
    w1_ref[...] = total.astype(BF16)
    rows_out[...] = rows_ref[...]


def second_weights(second_ref, bias_ref, head_ref, w2_ref, head_out):
    rows = CH * BAND
    row_r = iota((rows, K2), 0) % BAND
    col = iota((rows, K2), 1)
    col_r = col % 160 // CH
    spread = (iota((rows, CH), 0) // BAND == iota((rows, CH), 1)).astype(F32).astype(BF16)
    f_c = iota((CH, K2), 0)
    f_col = iota((CH, K2), 1)
    second = second_ref[...].reshape(9 * CH, CH)
    by_dw = [
        dot(second, ((f_col // 160 == dw) & (f_col % CH == f_c)).astype(F32).astype(BF16)) for dw in range(3)
    ]
    total = jnp.zeros((rows, K2), F32)
    for a in range(3):
        picked = sum(by_dw[dw][(3 * a + dw) * CH : (3 * a + dw + 1) * CH] for dw in range(3))
        total = total + jnp.where(col_r - row_r == a, dot(spread, picked.astype(BF16)), 0.0)
    total = jnp.where(col >= 480, 0.0, total)
    spread_bias = iota((rows, CH), 0) // BAND == iota((rows, CH), 1)
    for k, piece in enumerate(pieces(bias_ref[...])):
        total = jnp.where(col == 480 + k, column(piece.astype(F32), spread_bias), total)
    w2_ref[...] = total.astype(BF16)
    head_out[...] = jnp.broadcast_to(column(head_ref[...], spread_bias), (rows, LANES))


def weights_kernel(first_ref, first_bias_ref, rows_ref, second_ref, second_bias_ref, head_ref, *outs):
    first_weights(first_ref, first_bias_ref, rows_ref, *outs[:2])
    second_weights(second_ref, second_bias_ref, head_ref, *outs[2:])


def exchanges(borders, deep):
    order = [[(k, k + 1), (k + 1, k)] for k in range(borders)]
    if deep and borders > 1:
        order[0] = [(1, 0), (2, 1)]
        order[1] = [(0, 1), (1, 2)]
    return order


def downward(borders):
    gy = lax.axis_index("gy")

    def member(pairs, down):
        found = False
        for i, j in pairs:
            if (j > i) == down:
                found = found | (gy == i)
        return found

    plain, deep = exchanges(borders, False), exchanges(borders, True)
    return [jnp.where(deep_half(), member(b, True), member(a, True)) for a, b in zip(plain, deep)]


def arrived(borders, above):
    gy = lax.axis_index("gy")

    def member(pairs):
        found = False
        for i, j in pairs:
            if (j > i) == above:
                found = found | (gy == j)
        return found

    plain, deep = exchanges(borders, False), exchanges(borders, True)
    return [jnp.where(deep_half(), member(b), member(a)) for a, b in zip(plain, deep)]


def packed(r0, r1):
    rows = [r[:, k * LANES : (k + 1) * LANES] for r in (r0, r1) for k in range(3)]
    rows = jnp.concatenate(rows + [jnp.zeros((2, LANES), F32)], axis=0)
    return jnp.concatenate([rows, rows], axis=0)


def unpacked(block, at):
    r0, r1 = (jnp.concatenate([block[k + j : k + j + 1] for j in range(3)], axis=1) for k in (0, 3))
    zeros = [jnp.zeros((n, RING), F32) for n in (at, 6 - at)]
    return jnp.concatenate([x for x in (zeros[0], r0, r1, zeros[1]) if x.shape[0]], axis=0)


def sides_kernel(own_ref, core_ref, chip_ref, sides_ref, *slab_refs):
    odd = lax.axis_index("gx") % 2 == 1
    first = iota((16, LANES), 1) < LANES // 2
    ends = {}
    for r in range(0, TILE, 16):
        core, chip = core_ref[r : r + 16, :].astype(F32), chip_ref[r : r + 16, :].astype(F32)
        left = jnp.where(odd, core[:, LANES:], chip[:, LANES:])
        right = jnp.where(odd, chip[:, :LANES], core[:, :LANES])
        side = jnp.where(first, right, left)
        sides_ref[r : r + 16, :] = side.astype(BF16)
        if r in (0, TILE - 16):
            ring = jnp.concatenate([own_ref[r : r + 16, :].astype(F32), side], axis=1)
            ends[r] = packed(ring[0:1], ring[1:2]) if r == 0 else packed(ring[14:15], ring[15:16])
    for slab_ref, down in zip(slab_refs, downward(len(slab_refs))):
        slab_ref[...] = jnp.where(down, ends[TILE - 16], ends[0]).astype(BF16)


def around(ring):
    return [pltpu.roll(ring, 1, 1), ring, pltpu.roll(ring, RING - 1, 1)]


def ones_rows():
    return jnp.where(iota((16, TILE), 0) < 3, 1.0, 0.0).astype(BF16)


def add_up(parts):
    while len(parts) > 1:
        parts = [parts[i] + parts[i + 1] for i in range(0, len(parts), 2)]
    return parts[0]


def stage(raw_ref, start, ring):
    for k, x in enumerate(around(ring)):
        raw_ref[k, start : start + ring.shape[0], :] = x


def stage_own(raw_ref, own_ref, sides_ref):
    for r in range(0, TILE, 16):
        rows = slice(r, r + 16)
        ring = jnp.concatenate([own_ref[rows, :].astype(F32), sides_ref[rows, :].astype(F32)], axis=1)
        stage(raw_ref, BAND + r, ring)


def first_bands(bands, w1_ref, rows_ref, raw_ref, hid_ref):
    size = BAND * CH

    def grid(j):
        kind = 16 * (1 if j == 0 else 2 if j == BANDS else 0)
        raw = [raw_ref[k, BAND * j : BAND * j + 16, :].astype(BF16) for k in range(3)]
        return jnp.concatenate(raw * 3 + [rows_ref[kind : kind + 16, :]], axis=0)

    def keep(j, ring):
        for dw, x in enumerate(around(ring)):
            hid_ref[dw, j * size : (j + 1) * size, :] = x[:, :TILE]

    bands = list(bands)
    while bands:
        now, bands = bands[:2], bands[2:]
        grids = [grid(j) for j in now]
        if len(now) == 2:
            grids[1] = jnp.concatenate([grids[1][:, TILE:], grids[1][:, :TILE]], axis=1)
        found = jnp.maximum(dot(w1_ref[...], jnp.concatenate(grids, axis=1)), 0.0).astype(BF16)
        keep(now[0], found[:, :RING])
        if len(now) == 2:
            keep(now[1], jnp.concatenate([found[:, RING + LANES :], found[:, RING : RING + LANES]], axis=1))


def second_bands(bands, w2_ref, head_ref, raw_ref, hid_ref, res_ref):
    tail = jnp.concatenate([ones_rows(), jnp.zeros((16, TILE), BF16)], axis=0)
    bands = list(bands)
    while bands:
        now, bands = bands[:2], bands[2:]
        grids = []
        for b in now:
            start = (b * BAND + 6) * CH
            grids.append(jnp.concatenate([hid_ref[dw, start : start + 160, :] for dw in range(3)] + [tail], axis=0))
        deep = jnp.maximum(dot(w2_ref[...], jnp.concatenate(grids, axis=1)), 0.0)
        deep = deep * jnp.concatenate([head_ref[...]] * (2 * len(now)), axis=1)
        total = add_up([deep[o * BAND : (o + 1) * BAND] for o in range(CH)])
        for n, b in enumerate(now):
            center = raw_ref[1, BAND * (b + 1) : BAND * (b + 2), :TILE]
            res_ref[b * BAND : (b + 1) * BAND, :] = center + total[:, n * TILE : (n + 1) * TILE]


def inner_rows(own_ref, sides_ref, w1_ref, rows_ref, w2_ref, head_ref, outs, room):
    size = BAND * CH
    out_ref, top_ref, bottom_ref = outs
    raw_ref, hid_ref, res_ref = room
    stage_own(raw_ref, own_ref, sides_ref)
    for k in range(3):
        raw_ref[k, BAND + TILE :, :] = jnp.zeros((BAND, RING), F32)
    first_bands(range(1, BANDS + 1), w1_ref, rows_ref, raw_ref, hid_ref)
    top_ref[...] = hid_ref[:, size : 2 * size, :]
    bottom_ref[...] = hid_ref[:, BANDS * size - 2 * CH : (BANDS + 1) * size - 2 * CH, :]
    second_bands(range(1, BANDS - 1), w2_ref, head_ref, raw_ref, hid_ref, res_ref)
    res_ref[0:BAND, :] = jnp.zeros((BAND, TILE), F32)
    res_ref[TILE - BAND :, :] = jnp.zeros((BAND, TILE), F32)
    out_ref[...] = res_ref[...].astype(BF16)


def early_kernel(*refs):
    ins, refs = refs[:6], refs[6:]
    count = (len(refs) - 6) // 2
    slabs, outs, slab_outs, room = refs[:count], refs[count : count + 3], refs[count + 3 : -3], refs[-3:]

    @pl.when(early())
    def _():
        inner_rows(*ins, outs, room)

    for slab, out in zip(slabs, slab_outs):
        out[...] = slab[...]


def inner_kernel(*refs):
    @pl.when(waits() & jnp.logical_not(early()))
    def _():
        inner_rows(*refs[:6], refs[9:12], refs[12:])


def border(border_refs, above):
    value = jnp.zeros((16, LANES), F32)
    for ref, here in zip(border_refs, arrived(len(border_refs), above)):
        value = jnp.where(here, ref[...].astype(F32), value)
    return value


def outer_kernel(
    own_ref,
    sides_ref,
    w1_ref,
    rows_ref,
    w2_ref,
    head_ref,
    inner_ref,
    top_ref,
    bottom_ref,
    *refs,
):
    borders, (out_ref, raw_ref, hid_ref, res_ref) = refs[:-4], refs[-4:]
    gy = lax.axis_index("gy")
    size = BAND * CH

    def above():
        return unpacked(border(borders, True), 6)

    def below():
        return unpacked(border(borders, False), 0)

    @pl.when(jnp.logical_not(waits()))
    def _():
        stage(raw_ref, 0, above())
        stage(raw_ref, BAND + TILE, below())
        stage_own(raw_ref, own_ref, sides_ref)
        first_bands(range(BANDS + 1), w1_ref, rows_ref, raw_ref, hid_ref)
        second_bands(range(BANDS), w2_ref, head_ref, raw_ref, hid_ref, res_ref)
        out_ref[...] = res_ref[...].astype(BF16)

    @pl.when(waits())
    def _():
        first, last = slice(0, 16), slice(TILE - 16, TILE)
        own = own_ref[first, :].astype(F32)[0:8], own_ref[last, :].astype(F32)[8:16]
        side = sides_ref[first, :].astype(F32)[0:8], sides_ref[last, :].astype(F32)[8:16]
        near = [jnp.concatenate(pair, axis=1) for pair in zip(own, side)]
        grids = []
        for ring, rows in (
            (jnp.concatenate([above(), near[0]], axis=0), rows_ref[16:32, :]),
            (jnp.concatenate([near[1], below()], axis=0), rows_ref[32:48, :]),
        ):
            grids.append(jnp.concatenate([x.astype(BF16) for x in around(ring)] * 3 + [rows], axis=0))
        found = jnp.maximum(dot(w1_ref[size - 2 * CH :, :], jnp.concatenate(grids, axis=1)), 0.0)
        found = [[x[:, :TILE].astype(BF16) for x in around(found[:, n * RING : (n + 1) * RING])] for n in range(2)]
        hidden = []
        for dw in range(3):
            upper = jnp.concatenate([found[0][dw], top_ref[dw]], axis=0)
            lower = jnp.concatenate([bottom_ref[dw], found[1][dw]], axis=0)
            hidden.append(jnp.concatenate([upper, lower], axis=1))
        tail = jnp.concatenate([ones_rows(), jnp.zeros((16, TILE), BF16)], axis=0)
        hidden.append(jnp.concatenate([tail, tail], axis=1))
        deep = jnp.maximum(dot(w2_ref[...], jnp.concatenate(hidden, axis=0)), 0.0)
        deep = deep * jnp.concatenate([head_ref[...]] * 4, axis=1)
        total = add_up([deep[o * BAND : (o + 1) * BAND] for o in range(CH)])
        upper = own[0] + total[:, :TILE]
        lower = own[1] + total[:, TILE:]
        out_ref[first, :] = jnp.concatenate([upper, inner_ref[first, :].astype(F32)[8:16]], axis=0).astype(BF16)
        out_ref[last, :] = jnp.concatenate([inner_ref[last, :].astype(F32)[0:8], lower], axis=0).astype(BF16)


def transform(image_ref, across_ref, down_ref):
    halves = [
        dot(image_ref[:, q * PATCH : (q + 1) * PATCH], across_ref[...]).astype(BF16) for q in range(2)
    ]
    results = []
    for a in range(2):
        rows = slice(a * PATCH, (a + 1) * PATCH)
        cos_rows = jnp.concatenate([h[rows, :PATCH] for h in halves], axis=1)
        sin_rows = jnp.concatenate([h[rows, PATCH:] for h in halves], axis=1)
        both = dot(down_ref[...], jnp.concatenate([cos_rows, sin_rows], axis=0))
        results.append((both[:PATCH], both[PATCH:]))
    return results


def own_kernel(image_ref, across_ref, down_ref, out_ref):
    for a, (real, imag) in enumerate(transform(image_ref, across_ref, down_ref)):
        rows = slice(a * PATCH, (a + 1) * PATCH)
        out_ref[0, rows, :] = real
        out_ref[1, rows, :] = imag


def cross_kernel(image_ref, across_ref, down_ref, own_ref, out_ref, held_ref, sems):
    copies = []
    for a, (real, imag) in enumerate(transform(image_ref, across_ref, down_ref)):
        rows = slice(a * PATCH, (a + 1) * PATCH)
        own_real, own_imag = own_ref[0, rows, :], own_ref[1, rows, :]
        for part, value in enumerate(
            (own_real * real + own_imag * imag, own_imag * real - own_real * imag)
        ):
            held_ref[part, rows, :] = value
            copies.append(
                pltpu.make_async_copy(held_ref.at[part, rows], out_ref.at[0, part, rows], sems.at[a, part])
            )
            copies[-1].start()
    for copy in copies:
        copy.wait()


def full(shape):
    return pl.BlockSpec(shape, lambda: (0,) * len(shape), memory_space=VMEM)


def call(kernel, name, out_shape, args, scratch=(), flops=0, in_specs=None, out_specs=None, aliases=None):
    return pl.pallas_call(
        kernel,
        name=name,
        out_shape=out_shape,
        in_specs=in_specs or [full(a.shape) for a in args],
        out_specs=out_specs or jax.tree.map(lambda o: full(o.shape), out_shape),
        input_output_aliases=aliases or {},
        scratch_shapes=list(scratch),
        compiler_params=PARAMS,
        cost_estimate=pl.CostEstimate(flops=flops, bytes_accessed=0, transcendentals=0),
    )(*args)


def shaped(*shape, dtype=BF16):
    return jax.ShapeDtypeStruct(shape, dtype)


WEIGHTS = (
    shaped(BAND * CH, K1),
    shaped(48, RING),
    shaped(CH * BAND, K2),
    shaped(CH * BAND, LANES, dtype=F32),
)
ROOM = (
    pltpu.VMEM((3, TILE + 2 * BAND, RING), F32),
    pltpu.VMEM((3, (BANDS + 1) * BAND * CH, TILE), BF16),
    pltpu.VMEM((TILE, TILE), F32),
)


def prepare(first, first_bias, second, second_bias, head):
    rows = call(last_rows_kernel, "last_rows", WEIGHTS[1], (), flops=1 << 31)
    given = (first, first_bias, rows, second, second_bias, head)
    return call(weights_kernel, "weights", WEIGHTS, given)


def sides(own, core, chip, borders):
    slab = shaped(16, LANES)
    shapes = (shaped(TILE, LANES),) + (slab,) * borders
    return call(sides_kernel, "sides", shapes, (own, core, chip))


INSIDE = (shaped(TILE, TILE), shaped(3, BAND * CH, TILE), shaped(3, BAND * CH, TILE))


def inner_early(own, side, weights, slabs):
    shapes = INSIDE + (shaped(16, LANES),) * len(slabs)
    outs = call(early_kernel, "early_rows", shapes, (own, side, *weights, *slabs), scratch=ROOM)
    return outs[:3], outs[3:]


def inner(own, side, weights, inside):
    args = (own, side, *weights, *inside)
    return call(
        inner_kernel, "inner_rows", INSIDE, args, scratch=ROOM, flops=3 << 30, aliases={6: 0, 7: 1, 8: 2}
    )


def outer(own, side, weights, inside, borders):
    return call(
        outer_kernel,
        "outer_rows",
        shaped(TILE, TILE),
        (own, side, *weights, *inside, *borders),
        scratch=ROOM,
        flops=3 << 30,
        aliases={6: 0},
    )


def own_spectrum(image, across, down):
    return call(
        own_kernel, "own_spectrum", shaped(2, TILE, TILE, dtype=F32), (image, across, down), flops=1 << 29
    )


def cross_spectrum(image, across, down, own):
    return call(
        cross_kernel,
        "cross_spectrum",
        shaped(1, 2, TILE, TILE, dtype=F32),
        (image, across, down, own),
        scratch=[pltpu.VMEM((2, TILE, TILE), F32), pltpu.SemaphoreType.DMA((2, 2))],
        flops=1 << 29,
        out_specs=pl.BlockSpec(memory_space=pl.ANY),
    )


def from_step(value, axis, step):
    count = lax.axis_size(axis)
    pairs = [(i, i + step) for i in range(count) if 0 <= i + step < count]
    return lax.ppermute(value, axis, pairs)


def swap(value, axis, starts):
    pairs = [(i, i + 1) for i in starts]
    return lax.ppermute(value, axis, pairs + [(j, i) for i, j in pairs])


def exchange(slab, place):
    depth, rows = lax.axis_size("gz"), lax.axis_size("gy")
    pairs = []
    for z in range(depth):
        for i, j in exchanges(rows - 1, z >= depth // 2)[place]:
            pairs.append((z * rows + i, z * rows + j))
    return lax.ppermute(slab, ("gz", "gy"), pairs)


def on_device(section, first_kernel, first_bias, second_kernel, second_bias, head_weight):
    own = section[0]
    columns, rows = lax.axis_size("gx"), lax.axis_size("gy")
    chip = swap(own, "gx", range(1, columns - 1, 2))
    core = swap(own, "gx", range(0, columns - 1, 2))
    given = (first_kernel, first_bias[None], second_kernel, second_bias[None], head_weight[None])
    weights = prepare(*given)
    side, *slabs = sides(own, core, chip, rows - 1)
    inside, slabs = inner_early(own, side, weights, slabs)
    borders = [exchange(slab, k) for k, slab in enumerate(slabs)]
    inside = inner(own, side, weights, inside)
    restored = outer(own, side, weights, inside, borders)
    across, down = dft_tables()
    later = from_step(restored, "gz", -1)
    spectrum = own_spectrum(restored, across, down)
    return cross_spectrum(later, across, down, spectrum)


def solution(mesh):
    placed = (P("gz", "gy", "gx"), P(), P(), P(), P(), P())
    return jax.shard_map(
        on_device, mesh=mesh, in_specs=placed, out_specs=P("gz", None, "gy", "gx"), check_vma=False
    )
```

```python
import math

import jax
import jax.numpy as jnp
import numpy as np
from jax import lax
from jax.experimental import pallas as pl
from jax.experimental.pallas import tpu as pltpu
from jax.sharding import PartitionSpec as P

PATCH = 128
TILE = 256
CH = 16
BAND = 8
BANDS = TILE // BAND
LANES = 128
K1 = 160
RING = TILE + LANES
K2 = 512
FAR = -65536.0

F32 = jnp.float32
BF16 = jnp.bfloat16
VMEM = pltpu.MemorySpace.VMEM
SMEM = pltpu.MemorySpace.SMEM
PARAMS = pltpu.CompilerParams(vmem_limit_bytes=40 * 1024 * 1024)


def dft_tables():
    positions = np.arange(PATCH, dtype=np.int32)
    phase = positions[:, None] * positions[None, :] % PATCH
    angles = phase.astype(np.float32) * np.float32(2.0 * math.pi / PATCH)
    scaling = np.float32(1.0 / math.sqrt(PATCH))
    cosine = (np.cos(angles) * scaling).astype(BF16)
    sine = (np.sin(angles) * scaling).astype(BF16)
    across = np.concatenate([cosine, sine], axis=1)
    down = np.block([[cosine.T, -sine.T], [-sine.T, -cosine.T]]).astype(BF16)
    return across, down


def iota(shape, dim):
    return lax.broadcasted_iota(jnp.int32, shape, dim)


def dot(a, b):
    return lax.dot_general(a, b, (((1,), (0,)), ((), ())), preferred_element_type=F32)


def pieces(values):
    high = values.astype(BF16)
    rest = values - high.astype(F32)
    middle = rest.astype(BF16)
    low = (rest - middle.astype(F32)).astype(BF16)
    return high, middle, low


def column(row, spread):
    return jnp.sum(jnp.where(spread, row, 0.0), axis=1, keepdims=True)


def end_of(axis, last):
    return lax.axis_index(axis) == (lax.axis_size(axis) - 1 if last else 0)


def deep_half():
    return lax.axis_index("gz") >= lax.axis_size("gz") // 2


def early():
    return (lax.axis_index("gy") == 0) & deep_half()


def waits():
    return (lax.axis_index("gy") > 0) | deep_half()


def last_rows_kernel(rows_out):
    row = iota((16, RING), 0)
    lane = iota((16, RING), 1)
    keep = row < 3
    keep = keep | ((row == 3) & (lane == RING - 1) & end_of("gx", False))
    keep = keep | ((row == 3) & (lane == TILE) & end_of("gx", True))
    top = keep | ((row == 5) & end_of("gy", False))
    bottom = keep | ((row == 6) & end_of("gy", True))
    for k, mask in enumerate((keep, top, bottom)):
        rows_out[16 * k : 16 * k + 16, :] = jnp.where(mask, 1.0, 0.0).astype(BF16)


def first_weights(first_ref, bias_ref, rows_ref, w1_ref, rows_out):
    rows = BAND * CH
    row_r = iota((rows, K1), 0) // CH
    col = iota((rows, K1), 1)
    col_i = col % 16
    stacked = jnp.concatenate(pieces(first_ref[...]), axis=0)
    spread = (iota((rows, 48), 0) % CH == iota((rows, 48), 1) % CH).astype(F32).astype(BF16)
    sel_t = iota((9, K1), 0)
    sel_col = iota((9, K1), 1)
    sel_b = sel_col % 48 // 16
    own_piece = iota((48, K1), 0) // CH == iota((48, K1), 1) // 48
    total = jnp.zeros((rows, K1), F32)
    for a in range(3):
        select = (sel_t == 3 * a + sel_b) & (sel_col < 144)
        picked = dot(stacked, select.astype(F32).astype(BF16))
        picked = jnp.where(own_piece, picked, 0.0).astype(BF16)
        total = total + jnp.where(col_i - row_r == a, dot(spread, picked), 0.0)
    spread_bias = iota((rows, CH), 0) % CH == iota((rows, CH), 1)
    total = jnp.where(col < 144, total, 0.0)
    for k, piece in enumerate(pieces(bias_ref[...])):
        total = jnp.where(col == 144 + k, column(piece.astype(F32), spread_bias), total)
    total = jnp.where(col == 147, FAR, total)
    total = jnp.where((col == 149) & (row_r < 7), FAR, total)
    total = jnp.where((col == 150) & (row_r == 7), FAR, total)
    w1_ref[...] = total.astype(BF16)
    rows_out[...] = rows_ref[...]


def second_weights(second_ref, bias_ref, head_ref, w2_ref, head_out):
    rows = CH * BAND
    row_r = iota((rows, K2), 0) % BAND
    col = iota((rows, K2), 1)
    col_r = col % 160 // CH
    spread = (iota((rows, CH), 0) // BAND == iota((rows, CH), 1)).astype(F32).astype(BF16)
    f_c = iota((CH, K2), 0)
    f_col = iota((CH, K2), 1)
    second = second_ref[...].reshape(9 * CH, CH)
    by_dw = [
        dot(second, ((f_col // 160 == dw) & (f_col % CH == f_c)).astype(F32).astype(BF16)) for dw in range(3)
    ]
    total = jnp.zeros((rows, K2), F32)
    for a in range(3):
        picked = sum(by_dw[dw][(3 * a + dw) * CH : (3 * a + dw + 1) * CH] for dw in range(3))
        total = total + jnp.where(col_r - row_r == a, dot(spread, picked.astype(BF16)), 0.0)
    total = jnp.where(col >= 480, 0.0, total)
    spread_bias = iota((rows, CH), 0) // BAND == iota((rows, CH), 1)
    for k, piece in enumerate(pieces(bias_ref[...])):
        total = jnp.where(col == 480 + k, column(piece.astype(F32), spread_bias), total)
    w2_ref[...] = total.astype(BF16)
    head_out[...] = jnp.broadcast_to(column(head_ref[...], spread_bias), (rows, LANES))


def weights_kernel(first_ref, first_bias_ref, rows_ref, second_ref, second_bias_ref, head_ref, *outs):
    first_weights(first_ref, first_bias_ref, rows_ref, *outs[:2])
    second_weights(second_ref, second_bias_ref, head_ref, *outs[2:])


def exchanges(borders, deep):
    order = [[(k, k + 1), (k + 1, k)] for k in range(borders)]
    if deep and borders > 1:
        order[0] = [(1, 0), (2, 1)]
        order[1] = [(0, 1), (1, 2)]
    return order


def downward(borders):
    gy = lax.axis_index("gy")

    def member(pairs, down):
        found = False
        for i, j in pairs:
            if (j > i) == down:
                found = found | (gy == i)
        return found

    plain, deep = exchanges(borders, False), exchanges(borders, True)
    return [jnp.where(deep_half(), member(b, True), member(a, True)) for a, b in zip(plain, deep)]


def arrived(borders, above):
    gy = lax.axis_index("gy")

    def member(pairs):
        found = False
        for i, j in pairs:
            if (j > i) == above:
                found = found | (gy == j)
        return found

    plain, deep = exchanges(borders, False), exchanges(borders, True)
    return [jnp.where(deep_half(), member(b), member(a)) for a, b in zip(plain, deep)]


def packed(r0, r1):
    rows = [r[:, k * LANES : (k + 1) * LANES] for r in (r0, r1) for k in range(3)]
    rows = jnp.concatenate(rows + [jnp.zeros((2, LANES), F32)], axis=0)
    return jnp.concatenate([rows, rows], axis=0)


def unpacked(block, at):
    r0, r1 = (jnp.concatenate([block[k + j : k + j + 1] for j in range(3)], axis=1) for k in (0, 3))
    zeros = [jnp.zeros((n, RING), F32) for n in (at, 6 - at)]
    return jnp.concatenate([x for x in (zeros[0], r0, r1, zeros[1]) if x.shape[0]], axis=0)


def sides_kernel(own_ref, core_ref, chip_ref, sides_ref, *slab_refs):
    odd = lax.axis_index("gx") % 2 == 1
    first = iota((16, LANES), 1) < LANES // 2
    ends = {}
    for r in range(0, TILE, 16):
        core, chip = core_ref[r : r + 16, :].astype(F32), chip_ref[r : r + 16, :].astype(F32)
        left = jnp.where(odd, core[:, LANES:], chip[:, LANES:])
        right = jnp.where(odd, chip[:, :LANES], core[:, :LANES])
        side = jnp.where(first, right, left)
        sides_ref[r : r + 16, :] = side.astype(BF16)
        if r in (0, TILE - 16):
            ring = jnp.concatenate([own_ref[r : r + 16, :].astype(F32), side], axis=1)
            ends[r] = packed(ring[0:1], ring[1:2]) if r == 0 else packed(ring[14:15], ring[15:16])
    for slab_ref, down in zip(slab_refs, downward(len(slab_refs))):
        slab_ref[...] = jnp.where(down, ends[TILE - 16], ends[0]).astype(BF16)


def around(ring):
    return [pltpu.roll(ring, 1, 1), ring, pltpu.roll(ring, RING - 1, 1)]


def ones_rows():
    return jnp.where(iota((16, TILE), 0) < 3, 1.0, 0.0).astype(BF16)


def add_up(parts):
    while len(parts) > 1:
        parts = [parts[i] + parts[i + 1] for i in range(0, len(parts), 2)]
    return parts[0]


def stage(raw_ref, start, ring):
    for k, x in enumerate(around(ring)):
        raw_ref[k, start : start + ring.shape[0], :] = x


def stage_own(raw_ref, own_ref, sides_ref):
    for r in range(0, TILE, 16):
        rows = slice(r, r + 16)
        ring = jnp.concatenate([own_ref[rows, :].astype(F32), sides_ref[rows, :].astype(F32)], axis=1)
        stage(raw_ref, BAND + r, ring)


def first_bands(bands, w1_ref, rows_ref, raw_ref, hid_ref):
    size = BAND * CH

    def grid(j):
        kind = 16 * (1 if j == 0 else 2 if j == BANDS else 0)
        raw = [raw_ref[k, BAND * j : BAND * j + 16, :].astype(BF16) for k in range(3)]
        return jnp.concatenate(raw * 3 + [rows_ref[kind : kind + 16, :]], axis=0)

    def keep(j, ring):
        for dw, x in enumerate(around(ring)):
            hid_ref[dw, j * size : (j + 1) * size, :] = x[:, :TILE]

    bands = list(bands)
    while bands:
        now, bands = bands[:2], bands[2:]
        grids = [grid(j) for j in now]
        if len(now) == 2:
            grids[1] = jnp.concatenate([grids[1][:, TILE:], grids[1][:, :TILE]], axis=1)
        found = jnp.maximum(dot(w1_ref[...], jnp.concatenate(grids, axis=1)), 0.0).astype(BF16)
        keep(now[0], found[:, :RING])
        if len(now) == 2:
            keep(now[1], jnp.concatenate([found[:, RING + LANES :], found[:, RING : RING + LANES]], axis=1))


def second_bands(bands, w2_ref, head_ref, raw_ref, hid_ref, res_ref):
    tail = jnp.concatenate([ones_rows(), jnp.zeros((16, TILE), BF16)], axis=0)
    bands = list(bands)
    while bands:
        now, bands = bands[:2], bands[2:]
        grids = []
        for b in now:
            start = (b * BAND + 6) * CH
            grids.append(jnp.concatenate([hid_ref[dw, start : start + 160, :] for dw in range(3)] + [tail], axis=0))
        deep = jnp.maximum(dot(w2_ref[...], jnp.concatenate(grids, axis=1)), 0.0)
        deep = deep * jnp.concatenate([head_ref[...]] * (2 * len(now)), axis=1)
        total = add_up([deep[o * BAND : (o + 1) * BAND] for o in range(CH)])
        for n, b in enumerate(now):
            center = raw_ref[1, BAND * (b + 1) : BAND * (b + 2), :TILE]
            res_ref[b * BAND : (b + 1) * BAND, :] = center + total[:, n * TILE : (n + 1) * TILE]


def inner_rows(own_ref, sides_ref, w1_ref, rows_ref, w2_ref, head_ref, outs, room):
    size = BAND * CH
    out_ref, top_ref, bottom_ref = outs
    raw_ref, hid_ref, res_ref = room
    stage_own(raw_ref, own_ref, sides_ref)
    for k in range(3):
        raw_ref[k, BAND + TILE :, :] = jnp.zeros((BAND, RING), F32)
    first_bands(range(1, BANDS + 1), w1_ref, rows_ref, raw_ref, hid_ref)
    top_ref[...] = hid_ref[:, size : 2 * size, :]
    bottom_ref[...] = hid_ref[:, BANDS * size - 2 * CH : (BANDS + 1) * size - 2 * CH, :]
    second_bands(range(1, BANDS - 1), w2_ref, head_ref, raw_ref, hid_ref, res_ref)
    res_ref[0:BAND, :] = jnp.zeros((BAND, TILE), F32)
    res_ref[TILE - BAND :, :] = jnp.zeros((BAND, TILE), F32)
    out_ref[...] = res_ref[...].astype(BF16)


def early_kernel(*refs):
    ins, refs = refs[:6], refs[6:]
    count = (len(refs) - 6) // 2
    slabs, outs, slab_outs, room = refs[:count], refs[count : count + 3], refs[count + 3 : -3], refs[-3:]

    @pl.when(early())
    def _():
        inner_rows(*ins, outs, room)

    for slab, out in zip(slabs, slab_outs):
        out[...] = slab[...]


def inner_kernel(*refs):
    @pl.when(waits() & jnp.logical_not(early()))
    def _():
        inner_rows(*refs[:6], refs[9:12], refs[12:])

    @pl.when(early())
    def _():
        for found, out in zip(refs[6:9], refs[9:12]):
            out[...] = found[...]


def border(border_refs, above):
    value = jnp.zeros((16, LANES), F32)
    for ref, here in zip(border_refs, arrived(len(border_refs), above)):
        value = jnp.where(here, ref[...].astype(F32), value)
    return value


def outer_kernel(
    own_ref,
    sides_ref,
    w1_ref,
    rows_ref,
    w2_ref,
    head_ref,
    inner_ref,
    top_ref,
    bottom_ref,
    *refs,
):
    borders, (out_ref, raw_ref, hid_ref, res_ref) = refs[:-4], refs[-4:]
    gy = lax.axis_index("gy")
    size = BAND * CH

    def above():
        return unpacked(border(borders, True), 6)

    def below():
        return unpacked(border(borders, False), 0)

    @pl.when(jnp.logical_not(waits()))
    def _():
        stage(raw_ref, 0, above())
        stage(raw_ref, BAND + TILE, below())
        stage_own(raw_ref, own_ref, sides_ref)
        first_bands(range(BANDS + 1), w1_ref, rows_ref, raw_ref, hid_ref)
        second_bands(range(BANDS), w2_ref, head_ref, raw_ref, hid_ref, res_ref)
        out_ref[...] = res_ref[...].astype(BF16)

    @pl.when(waits())
    def _():
        first, last = slice(0, 16), slice(TILE - 16, TILE)
        out_ref[16 : TILE - 16, :] = inner_ref[16 : TILE - 16, :]
        own = own_ref[first, :].astype(F32)[0:8], own_ref[last, :].astype(F32)[8:16]
        side = sides_ref[first, :].astype(F32)[0:8], sides_ref[last, :].astype(F32)[8:16]
        near = [jnp.concatenate(pair, axis=1) for pair in zip(own, side)]
        grids = []
        for ring, rows in (
            (jnp.concatenate([above(), near[0]], axis=0), rows_ref[16:32, :]),
            (jnp.concatenate([near[1], below()], axis=0), rows_ref[32:48, :]),
        ):
            grids.append(jnp.concatenate([x.astype(BF16) for x in around(ring)] * 3 + [rows], axis=0))
        found = jnp.maximum(dot(w1_ref[size - 2 * CH :, :], jnp.concatenate(grids, axis=1)), 0.0)
        found = [[x[:, :TILE].astype(BF16) for x in around(found[:, n * RING : (n + 1) * RING])] for n in range(2)]
        hidden = []
        for dw in range(3):
            upper = jnp.concatenate([found[0][dw], top_ref[dw]], axis=0)
            lower = jnp.concatenate([bottom_ref[dw], found[1][dw]], axis=0)
            hidden.append(jnp.concatenate([upper, lower], axis=1))
        tail = jnp.concatenate([ones_rows(), jnp.zeros((16, TILE), BF16)], axis=0)
        hidden.append(jnp.concatenate([tail, tail], axis=1))
        deep = jnp.maximum(dot(w2_ref[...], jnp.concatenate(hidden, axis=0)), 0.0)
        deep = deep * jnp.concatenate([head_ref[...]] * 4, axis=1)
        total = add_up([deep[o * BAND : (o + 1) * BAND] for o in range(CH)])
        upper = own[0] + total[:, :TILE]
        lower = own[1] + total[:, TILE:]
        out_ref[first, :] = jnp.concatenate([upper, inner_ref[first, :].astype(F32)[8:16]], axis=0).astype(BF16)
        out_ref[last, :] = jnp.concatenate([inner_ref[last, :].astype(F32)[0:8], lower], axis=0).astype(BF16)


def transform(image_ref, across_ref, down_ref):
    halves = [
        dot(image_ref[:, q * PATCH : (q + 1) * PATCH], across_ref[...]).astype(BF16) for q in range(2)
    ]
    results = []
    for a in range(2):
        rows = slice(a * PATCH, (a + 1) * PATCH)
        cos_rows = jnp.concatenate([h[rows, :PATCH] for h in halves], axis=1)
        sin_rows = jnp.concatenate([h[rows, PATCH:] for h in halves], axis=1)
        both = dot(down_ref[...], jnp.concatenate([cos_rows, sin_rows], axis=0))
        results.append((both[:PATCH], both[PATCH:]))
    return results


def own_kernel(image_ref, across_ref, down_ref, out_ref):
    for a, (real, imag) in enumerate(transform(image_ref, across_ref, down_ref)):
        rows = slice(a * PATCH, (a + 1) * PATCH)
        out_ref[0, rows, :] = real
        out_ref[1, rows, :] = imag


def cross_kernel(image_ref, across_ref, down_ref, own_ref, out_ref, held_ref, sems):
    copies = []
    for a, (real, imag) in enumerate(transform(image_ref, across_ref, down_ref)):
        rows = slice(a * PATCH, (a + 1) * PATCH)
        own_real, own_imag = own_ref[0, rows, :], own_ref[1, rows, :]
        for part, value in enumerate(
            (own_real * real + own_imag * imag, own_imag * real - own_real * imag)
        ):
            held_ref[part, rows, :] = value
            copies.append(
                pltpu.make_async_copy(held_ref.at[part, rows], out_ref.at[0, part, rows], sems.at[a, part])
            )
            copies[-1].start()
    for copy in copies:
        copy.wait()


def full(shape):
    return pl.BlockSpec(shape, lambda: (0,) * len(shape), memory_space=VMEM)


def call(kernel, name, out_shape, args, scratch=(), flops=0, in_specs=None, out_specs=None):
    return pl.pallas_call(
        kernel,
        name=name,
        out_shape=out_shape,
        in_specs=in_specs or [full(a.shape) for a in args],
        out_specs=out_specs or jax.tree.map(lambda o: full(o.shape), out_shape),
        scratch_shapes=list(scratch),
        compiler_params=PARAMS,
        cost_estimate=pl.CostEstimate(flops=flops, bytes_accessed=0, transcendentals=0),
    )(*args)


def shaped(*shape, dtype=BF16):
    return jax.ShapeDtypeStruct(shape, dtype)


WEIGHTS = (
    shaped(BAND * CH, K1),
    shaped(48, RING),
    shaped(CH * BAND, K2),
    shaped(CH * BAND, LANES, dtype=F32),
)
ROOM = (
    pltpu.VMEM((3, TILE + 2 * BAND, RING), F32),
    pltpu.VMEM((3, (BANDS + 1) * BAND * CH, TILE), BF16),
    pltpu.VMEM((TILE, TILE), F32),
)


def prepare(first, first_bias, second, second_bias, head):
    rows = call(last_rows_kernel, "last_rows", WEIGHTS[1], (), flops=1 << 31)
    given = (first, first_bias, rows, second, second_bias, head)
    return call(weights_kernel, "weights", WEIGHTS, given)


def sides(own, core, chip, borders):
    slab = shaped(16, LANES)
    shapes = (shaped(TILE, LANES),) + (slab,) * borders
    return call(sides_kernel, "sides", shapes, (own, core, chip))


INSIDE = (shaped(TILE, TILE), shaped(3, BAND * CH, TILE), shaped(3, BAND * CH, TILE))


def inner_early(own, side, weights, slabs):
    shapes = INSIDE + (shaped(16, LANES),) * len(slabs)
    outs = call(early_kernel, "early_rows", shapes, (own, side, *weights, *slabs), scratch=ROOM)
    return outs[:3], outs[3:]


def inner(own, side, weights, inside):
    args = (own, side, *weights, *inside)
    return call(
        inner_kernel, "inner_rows", INSIDE, args, scratch=ROOM, flops=3 << 30
    )


def outer(own, side, weights, inside, borders):
    return call(
        outer_kernel,
        "outer_rows",
        shaped(TILE, TILE),
        (own, side, *weights, *inside, *borders),
        scratch=ROOM,
        flops=3 << 30,
    )


def own_spectrum(image, across, down):
    return call(
        own_kernel, "own_spectrum", shaped(2, TILE, TILE, dtype=F32), (image, across, down), flops=1 << 29
    )


def cross_spectrum(image, across, down, own):
    return call(
        cross_kernel,
        "cross_spectrum",
        shaped(1, 2, TILE, TILE, dtype=F32),
        (image, across, down, own),
        scratch=[pltpu.VMEM((2, TILE, TILE), F32), pltpu.SemaphoreType.DMA((2, 2))],
        flops=1 << 29,
        out_specs=pl.BlockSpec(memory_space=pl.ANY),
    )


def from_step(value, axis, step):
    count = lax.axis_size(axis)
    pairs = [(i, i + step) for i in range(count) if 0 <= i + step < count]
    return lax.ppermute(value, axis, pairs)


def swap(value, axis, starts):
    pairs = [(i, i + 1) for i in starts]
    return lax.ppermute(value, axis, pairs + [(j, i) for i, j in pairs])


def exchange(slab, place):
    depth, rows = lax.axis_size("gz"), lax.axis_size("gy")
    pairs = []
    for z in range(depth):
        for i, j in exchanges(rows - 1, z >= depth // 2)[place]:
            pairs.append((z * rows + i, z * rows + j))
    return lax.ppermute(slab, ("gz", "gy"), pairs)


def on_device(section, first_kernel, first_bias, second_kernel, second_bias, head_weight):
    own = section[0]
    columns, rows = lax.axis_size("gx"), lax.axis_size("gy")
    chip = swap(own, "gx", range(1, columns - 1, 2))
    core = swap(own, "gx", range(0, columns - 1, 2))
    given = (first_kernel, first_bias[None], second_kernel, second_bias[None], head_weight[None])
    weights = prepare(*given)
    side, *slabs = sides(own, core, chip, rows - 1)
    inside, slabs = inner_early(own, side, weights, slabs)
    borders = [exchange(slab, k) for k, slab in enumerate(slabs)]
    inside = inner(own, side, weights, inside)
    restored = outer(own, side, weights, inside, borders)
    across, down = dft_tables()
    later = from_step(restored, "gz", -1)
    spectrum = own_spectrum(restored, across, down)
    return cross_spectrum(later, across, down, spectrum)


def solution(mesh):
    placed = (P("gz", "gy", "gx"), P(), P(), P(), P(), P())
    return jax.shard_map(
        on_device, mesh=mesh, in_specs=placed, out_specs=P("gz", None, "gy", "gx"), check_vma=False
    )
```

```python
import math

import jax
import jax.numpy as jnp
import numpy as np
from jax import lax
from jax.experimental import pallas as pl
from jax.experimental.pallas import tpu as pltpu
from jax.sharding import PartitionSpec as P

PATCH = 128
TILE = 256
CH = 16
BAND = 8
BANDS = TILE // BAND
LANES = 128
K1 = 160
RING = TILE + LANES
K2 = 512
FAR = -65536.0

F32 = jnp.float32
BF16 = jnp.bfloat16
VMEM = pltpu.MemorySpace.VMEM
SMEM = pltpu.MemorySpace.SMEM
PARAMS = pltpu.CompilerParams(vmem_limit_bytes=40 * 1024 * 1024)


def dft_tables():
    positions = np.arange(PATCH, dtype=np.int32)
    phase = positions[:, None] * positions[None, :] % PATCH
    angles = phase.astype(np.float32) * np.float32(2.0 * math.pi / PATCH)
    scaling = np.float32(1.0 / math.sqrt(PATCH))
    cosine = (np.cos(angles) * scaling).astype(BF16)
    sine = (np.sin(angles) * scaling).astype(BF16)
    across = np.concatenate([cosine, sine], axis=1)
    down = np.block([[cosine.T, -sine.T], [-sine.T, -cosine.T]]).astype(BF16)
    return across, down


def iota(shape, dim):
    return lax.broadcasted_iota(jnp.int32, shape, dim)


def dot(a, b):
    return lax.dot_general(a, b, (((1,), (0,)), ((), ())), preferred_element_type=F32)


def pieces(values):
    high = values.astype(BF16)
    rest = values - high.astype(F32)
    middle = rest.astype(BF16)
    low = (rest - middle.astype(F32)).astype(BF16)
    return high, middle, low


def column(row, spread):
    return jnp.sum(jnp.where(spread, row, 0.0), axis=1, keepdims=True)


def end_of(axis, last):
    return lax.axis_index(axis) == (lax.axis_size(axis) - 1 if last else 0)


def deep_half():
    return lax.axis_index("gz") >= lax.axis_size("gz") // 2


def early():
    return (lax.axis_index("gy") == 0) & deep_half()


def waits():
    return (lax.axis_index("gy") > 0) | deep_half()


def last_rows_kernel(rows_out):
    row = iota((16, RING), 0)
    lane = iota((16, RING), 1)
    keep = row < 3
    keep = keep | ((row == 3) & (lane == RING - 1) & end_of("gx", False))
    keep = keep | ((row == 3) & (lane == TILE) & end_of("gx", True))
    top = keep | ((row == 5) & end_of("gy", False))
    bottom = keep | ((row == 6) & end_of("gy", True))
    for k, mask in enumerate((keep, top, bottom)):
        rows_out[16 * k : 16 * k + 16, :] = jnp.where(mask, 1.0, 0.0).astype(BF16)


def first_weights(first_ref, bias_ref, rows_ref, w1_ref, rows_out):
    rows = BAND * CH
    row_r = iota((rows, K1), 0) // CH
    col = iota((rows, K1), 1)
    col_i = col % 16
    stacked = jnp.concatenate(pieces(first_ref[...]), axis=0)
    spread = (iota((rows, 48), 0) % CH == iota((rows, 48), 1) % CH).astype(F32).astype(BF16)
    sel_t = iota((9, K1), 0)
    sel_col = iota((9, K1), 1)
    sel_b = sel_col % 48 // 16
    own_piece = iota((48, K1), 0) // CH == iota((48, K1), 1) // 48
    total = jnp.zeros((rows, K1), F32)
    for a in range(3):
        select = (sel_t == 3 * a + sel_b) & (sel_col < 144)
        picked = dot(stacked, select.astype(F32).astype(BF16))
        picked = jnp.where(own_piece, picked, 0.0).astype(BF16)
        total = total + jnp.where(col_i - row_r == a, dot(spread, picked), 0.0)
    spread_bias = iota((rows, CH), 0) % CH == iota((rows, CH), 1)
    total = jnp.where(col < 144, total, 0.0)
    for k, piece in enumerate(pieces(bias_ref[...])):
        total = jnp.where(col == 144 + k, column(piece.astype(F32), spread_bias), total)
    total = jnp.where(col == 147, FAR, total)
    total = jnp.where((col == 149) & (row_r < 7), FAR, total)
    total = jnp.where((col == 150) & (row_r == 7), FAR, total)
    w1_ref[...] = total.astype(BF16)
    rows_out[...] = rows_ref[...]


def second_weights(second_ref, bias_ref, head_ref, w2_ref, head_out):
    rows = CH * BAND
    row_r = iota((rows, K2), 0) % BAND
    col = iota((rows, K2), 1)
    col_r = col % 160 // CH
    spread = (iota((rows, CH), 0) // BAND == iota((rows, CH), 1)).astype(F32).astype(BF16)
    f_c = iota((CH, K2), 0)
    f_col = iota((CH, K2), 1)
    second = second_ref[...].reshape(9 * CH, CH)
    by_dw = [
        dot(second, ((f_col // 160 == dw) & (f_col % CH == f_c)).astype(F32).astype(BF16)) for dw in range(3)
    ]
    total = jnp.zeros((rows, K2), F32)
    for a in range(3):
        picked = sum(by_dw[dw][(3 * a + dw) * CH : (3 * a + dw + 1) * CH] for dw in range(3))
        total = total + jnp.where(col_r - row_r == a, dot(spread, picked.astype(BF16)), 0.0)
    total = jnp.where(col >= 480, 0.0, total)
    spread_bias = iota((rows, CH), 0) // BAND == iota((rows, CH), 1)
    for k, piece in enumerate(pieces(bias_ref[...])):
        total = jnp.where(col == 480 + k, column(piece.astype(F32), spread_bias), total)
    w2_ref[...] = total.astype(BF16)
    head_out[...] = jnp.broadcast_to(column(head_ref[...], spread_bias), (rows, LANES))


def weights_kernel(first_ref, first_bias_ref, rows_ref, second_ref, second_bias_ref, head_ref, *outs):
    first_weights(first_ref, first_bias_ref, rows_ref, *outs[:2])
    second_weights(second_ref, second_bias_ref, head_ref, *outs[2:])


def exchanges(borders, deep):
    order = [[(k, k + 1), (k + 1, k)] for k in range(borders)]
    if deep and borders > 1:
        order[0] = [(1, 0), (2, 1)]
        order[1] = [(0, 1), (1, 2)]
    return order


def downward(borders):
    gy = lax.axis_index("gy")

    def member(pairs, down):
        found = False
        for i, j in pairs:
            if (j > i) == down:
                found = found | (gy == i)
        return found

    plain, deep = exchanges(borders, False), exchanges(borders, True)
    return [jnp.where(deep_half(), member(b, True), member(a, True)) for a, b in zip(plain, deep)]


def arrived(borders, above):
    gy = lax.axis_index("gy")

    def member(pairs):
        found = False
        for i, j in pairs:
            if (j > i) == above:
                found = found | (gy == j)
        return found

    plain, deep = exchanges(borders, False), exchanges(borders, True)
    return [jnp.where(deep_half(), member(b), member(a)) for a, b in zip(plain, deep)]


def packed(r0, r1):
    rows = [r[:, k * LANES : (k + 1) * LANES] for r in (r0, r1) for k in range(3)]
    rows = jnp.concatenate(rows + [jnp.zeros((2, LANES), F32)], axis=0)
    return jnp.concatenate([rows, rows], axis=0)


def unpacked(block, at):
    r0, r1 = (jnp.concatenate([block[k + j : k + j + 1] for j in range(3)], axis=1) for k in (0, 3))
    zeros = [jnp.zeros((n, RING), F32) for n in (at, 6 - at)]
    return jnp.concatenate([x for x in (zeros[0], r0, r1, zeros[1]) if x.shape[0]], axis=0)


def sides_kernel(own_ref, core_ref, chip_ref, sides_ref, *slab_refs):
    odd = lax.axis_index("gx") % 2 == 1
    first = iota((16, LANES), 1) < LANES // 2
    ends = {}
    for r in range(0, TILE, 16):
        core, chip = core_ref[r : r + 16, :].astype(F32), chip_ref[r : r + 16, :].astype(F32)
        left = jnp.where(odd, core[:, LANES:], chip[:, LANES:])
        right = jnp.where(odd, chip[:, :LANES], core[:, :LANES])
        side = jnp.where(first, right, left)
        sides_ref[r : r + 16, :] = side.astype(BF16)
        if r in (0, TILE - 16):
            ring = jnp.concatenate([own_ref[r : r + 16, :].astype(F32), side], axis=1)
            ends[r] = packed(ring[0:1], ring[1:2]) if r == 0 else packed(ring[14:15], ring[15:16])
    for slab_ref, down in zip(slab_refs, downward(len(slab_refs))):
        slab_ref[...] = jnp.where(down, ends[TILE - 16], ends[0]).astype(BF16)


def around(ring):
    return [pltpu.roll(ring, 1, 1), ring, pltpu.roll(ring, RING - 1, 1)]


def ones_rows():
    return jnp.where(iota((16, TILE), 0) < 3, 1.0, 0.0).astype(BF16)


def add_up(parts):
    while len(parts) > 1:
        parts = [parts[i] + parts[i + 1] for i in range(0, len(parts), 2)]
    return parts[0]


def stage(raw_ref, start, ring):
    for k, x in enumerate(around(ring)):
        raw_ref[k, start : start + ring.shape[0], :] = x


def stage_own(raw_ref, own_ref, sides_ref):
    for r in range(0, TILE, 16):
        rows = slice(r, r + 16)
        ring = jnp.concatenate([own_ref[rows, :].astype(F32), sides_ref[rows, :].astype(F32)], axis=1)
        stage(raw_ref, BAND + r, ring)


def first_bands(bands, w1_ref, rows_ref, raw_ref, hid_ref):
    size = BAND * CH

    def grid(j):
        kind = 16 * (1 if j == 0 else 2 if j == BANDS else 0)
        raw = [raw_ref[k, BAND * j : BAND * j + 16, :].astype(BF16) for k in range(3)]
        return jnp.concatenate(raw * 3 + [rows_ref[kind : kind + 16, :]], axis=0)

    def keep(j, ring):
        for dw, x in enumerate(around(ring)):
            hid_ref[dw, j * size : (j + 1) * size, :] = x[:, :TILE]

    bands = list(bands)
    while bands:
        now, bands = bands[:2], bands[2:]
        grids = [grid(j) for j in now]
        if len(now) == 2:
            grids[1] = jnp.concatenate([grids[1][:, TILE:], grids[1][:, :TILE]], axis=1)
        found = jnp.maximum(dot(w1_ref[...], jnp.concatenate(grids, axis=1)), 0.0).astype(BF16)
        keep(now[0], found[:, :RING])
        if len(now) == 2:
            keep(now[1], jnp.concatenate([found[:, RING + LANES :], found[:, RING : RING + LANES]], axis=1))


def second_bands(bands, w2_ref, head_ref, raw_ref, hid_ref, res_ref):
    tail = jnp.concatenate([ones_rows(), jnp.zeros((16, TILE), BF16)], axis=0)
    bands = list(bands)
    while bands:
        now, bands = bands[:2], bands[2:]
        grids = []
        for b in now:
            start = (b * BAND + 6) * CH
            grids.append(jnp.concatenate([hid_ref[dw, start : start + 160, :] for dw in range(3)] + [tail], axis=0))
        deep = jnp.maximum(dot(w2_ref[...], jnp.concatenate(grids, axis=1)), 0.0)
        deep = deep * jnp.concatenate([head_ref[...]] * (2 * len(now)), axis=1)
        total = add_up([deep[o * BAND : (o + 1) * BAND] for o in range(CH)])
        for n, b in enumerate(now):
            center = raw_ref[1, BAND * (b + 1) : BAND * (b + 2), :TILE]
            res_ref[b * BAND : (b + 1) * BAND, :] = center + total[:, n * TILE : (n + 1) * TILE]


def inner_rows(own_ref, sides_ref, w1_ref, rows_ref, w2_ref, head_ref, outs, room):
    size = BAND * CH
    out_ref, top_ref, bottom_ref = outs
    raw_ref, hid_ref, res_ref = room
    stage_own(raw_ref, own_ref, sides_ref)
    for k in range(3):
        raw_ref[k, BAND + TILE :, :] = jnp.zeros((BAND, RING), F32)
    first_bands(range(1, BANDS + 1), w1_ref, rows_ref, raw_ref, hid_ref)
    top_ref[...] = hid_ref[:, size : 2 * size, :]
    bottom_ref[...] = hid_ref[:, BANDS * size - 2 * CH : (BANDS + 1) * size - 2 * CH, :]
    second_bands(range(1, BANDS - 1), w2_ref, head_ref, raw_ref, hid_ref, res_ref)
    res_ref[0:BAND, :] = jnp.zeros((BAND, TILE), F32)
    res_ref[TILE - BAND :, :] = jnp.zeros((BAND, TILE), F32)
    out_ref[...] = res_ref[...].astype(BF16)


def early_kernel(*refs):
    ins, refs = refs[:6], refs[6:]
    count = (len(refs) - 6) // 2
    slabs, outs, slab_outs, room = refs[:count], refs[count : count + 3], refs[count + 3 : -3], refs[-3:]

    @pl.when(early())
    def _():
        inner_rows(*ins, outs, room)

    for slab, out in zip(slabs, slab_outs):
        out[...] = slab[...]


def inner_kernel(*refs):
    @pl.when(waits() & jnp.logical_not(early()))
    def _():
        inner_rows(*refs[:6], refs[9:12], refs[12:])

    @pl.when(early())
    def _():
        for found, out in zip(refs[6:9], refs[9:12]):
            out[...] = found[...]


def border(border_refs, above):
    value = jnp.zeros((16, LANES), F32)
    for ref, here in zip(border_refs, arrived(len(border_refs), above)):
        value = jnp.where(here, ref[...].astype(F32), value)
    return value


def outer_kernel(
    own_ref,
    sides_ref,
    w1_ref,
    rows_ref,
    w2_ref,
    head_ref,
    inner_ref,
    top_ref,
    bottom_ref,
    *refs,
):
    borders, (out_ref, raw_ref, hid_ref, res_ref) = refs[:-4], refs[-4:]
    gy = lax.axis_index("gy")
    size = BAND * CH

    def above():
        return unpacked(border(borders, True), 6)

    def below():
        return unpacked(border(borders, False), 0)

    @pl.when(jnp.logical_not(waits()))
    def _():
        stage(raw_ref, 0, above())
        stage(raw_ref, BAND + TILE, below())
        stage_own(raw_ref, own_ref, sides_ref)
        first_bands(range(BANDS + 1), w1_ref, rows_ref, raw_ref, hid_ref)
        second_bands(range(BANDS), w2_ref, head_ref, raw_ref, hid_ref, res_ref)
        out_ref[...] = res_ref[...].astype(BF16)

    @pl.when(waits())
    def _():
        first, last = slice(0, 16), slice(TILE - 16, TILE)
        out_ref[16 : TILE - 16, :] = inner_ref[16 : TILE - 16, :]
        own = own_ref[first, :].astype(F32)[0:8], own_ref[last, :].astype(F32)[8:16]
        side = sides_ref[first, :].astype(F32)[0:8], sides_ref[last, :].astype(F32)[8:16]
        near = [jnp.concatenate(pair, axis=1) for pair in zip(own, side)]
        grids = []
        for ring, rows in (
            (jnp.concatenate([above(), near[0]], axis=0), rows_ref[16:32, :]),
            (jnp.concatenate([near[1], below()], axis=0), rows_ref[32:48, :]),
        ):
            grids.append(jnp.concatenate([x.astype(BF16) for x in around(ring)] * 3 + [rows], axis=0))
        found = jnp.maximum(dot(w1_ref[size - 2 * CH :, :], jnp.concatenate(grids, axis=1)), 0.0)
        found = [[x[:, :TILE].astype(BF16) for x in around(found[:, n * RING : (n + 1) * RING])] for n in range(2)]
        hidden = []
        for dw in range(3):
            upper = jnp.concatenate([found[0][dw], top_ref[dw]], axis=0)
            lower = jnp.concatenate([bottom_ref[dw], found[1][dw]], axis=0)
            hidden.append(jnp.concatenate([upper, lower], axis=1))
        tail = jnp.concatenate([ones_rows(), jnp.zeros((16, TILE), BF16)], axis=0)
        hidden.append(jnp.concatenate([tail, tail], axis=1))
        deep = jnp.maximum(dot(w2_ref[...], jnp.concatenate(hidden, axis=0)), 0.0)
        deep = deep * jnp.concatenate([head_ref[...]] * 4, axis=1)
        total = add_up([deep[o * BAND : (o + 1) * BAND] for o in range(CH)])
        upper = own[0] + total[:, :TILE]
        lower = own[1] + total[:, TILE:]
        out_ref[first, :] = jnp.concatenate([upper, inner_ref[first, :].astype(F32)[8:16]], axis=0).astype(BF16)
        out_ref[last, :] = jnp.concatenate([inner_ref[last, :].astype(F32)[0:8], lower], axis=0).astype(BF16)


def transform(image_ref, across_ref, down_ref):
    halves = [
        dot(image_ref[:, q * PATCH : (q + 1) * PATCH], across_ref[...]).astype(BF16) for q in range(2)
    ]
    results = []
    for a in range(2):
        rows = slice(a * PATCH, (a + 1) * PATCH)
        cos_rows = jnp.concatenate([h[rows, :PATCH] for h in halves], axis=1)
        sin_rows = jnp.concatenate([h[rows, PATCH:] for h in halves], axis=1)
        both = dot(down_ref[...], jnp.concatenate([cos_rows, sin_rows], axis=0))
        results.append((both[:PATCH], both[PATCH:]))
    return results


def own_kernel(image_ref, across_ref, down_ref, out_ref):
    for a, (real, imag) in enumerate(transform(image_ref, across_ref, down_ref)):
        rows = slice(a * PATCH, (a + 1) * PATCH)
        out_ref[0, rows, :] = real
        out_ref[1, rows, :] = imag


def cross_kernel(image_ref, across_ref, down_ref, own_ref, out_ref, held_ref, sems):
    copies = []
    for a, (real, imag) in enumerate(transform(image_ref, across_ref, down_ref)):
        rows = slice(a * PATCH, (a + 1) * PATCH)
        own_real, own_imag = own_ref[0, rows, :], own_ref[1, rows, :]
        for part, value in enumerate(
            (own_real * real + own_imag * imag, own_imag * real - own_real * imag)
        ):
            held_ref[part, rows, :] = value
        copies.append(pltpu.make_async_copy(held_ref.at[:, rows], out_ref.at[0, :, rows], sems.at[a]))
        copies[-1].start()
    for copy in copies:
        copy.wait()


def full(shape):
    return pl.BlockSpec(shape, lambda: (0,) * len(shape), memory_space=VMEM)


def call(kernel, name, out_shape, args, scratch=(), flops=0, in_specs=None, out_specs=None):
    return pl.pallas_call(
        kernel,
        name=name,
        out_shape=out_shape,
        in_specs=in_specs or [full(a.shape) for a in args],
        out_specs=out_specs or jax.tree.map(lambda o: full(o.shape), out_shape),
        scratch_shapes=list(scratch),
        compiler_params=PARAMS,
        cost_estimate=pl.CostEstimate(flops=flops, bytes_accessed=0, transcendentals=0),
    )(*args)


def shaped(*shape, dtype=BF16):
    return jax.ShapeDtypeStruct(shape, dtype)


WEIGHTS = (
    shaped(BAND * CH, K1),
    shaped(48, RING),
    shaped(CH * BAND, K2),
    shaped(CH * BAND, LANES, dtype=F32),
)
ROOM = (
    pltpu.VMEM((3, TILE + 2 * BAND, RING), F32),
    pltpu.VMEM((3, (BANDS + 1) * BAND * CH, TILE), BF16),
    pltpu.VMEM((TILE, TILE), F32),
)


def prepare(first, first_bias, second, second_bias, head):
    rows = call(last_rows_kernel, "last_rows", WEIGHTS[1], (), flops=1 << 31)
    given = (first, first_bias, rows, second, second_bias, head)
    return call(weights_kernel, "weights", WEIGHTS, given)


def sides(own, core, chip, borders):
    slab = shaped(16, LANES)
    shapes = (shaped(TILE, LANES),) + (slab,) * borders
    return call(sides_kernel, "sides", shapes, (own, core, chip))


INSIDE = (shaped(TILE, TILE), shaped(3, BAND * CH, TILE), shaped(3, BAND * CH, TILE))


def inner_early(own, side, weights, slabs):
    shapes = INSIDE + (shaped(16, LANES),) * len(slabs)
    outs = call(early_kernel, "early_rows", shapes, (own, side, *weights, *slabs), scratch=ROOM)
    return outs[:3], outs[3:]


def inner(own, side, weights, inside):
    args = (own, side, *weights, *inside)
    return call(
        inner_kernel, "inner_rows", INSIDE, args, scratch=ROOM, flops=3 << 30
    )


def outer(own, side, weights, inside, borders):
    return call(
        outer_kernel,
        "outer_rows",
        shaped(TILE, TILE),
        (own, side, *weights, *inside, *borders),
        scratch=ROOM,
        flops=3 << 30,
    )


def own_spectrum(image, across, down):
    return call(
        own_kernel, "own_spectrum", shaped(2, TILE, TILE, dtype=F32), (image, across, down), flops=1 << 29
    )


def cross_spectrum(image, across, down, own):
    return call(
        cross_kernel,
        "cross_spectrum",
        shaped(1, 2, TILE, TILE, dtype=F32),
        (image, across, down, own),
        scratch=[pltpu.VMEM((2, TILE, TILE), F32), pltpu.SemaphoreType.DMA((2,))],
        flops=1 << 29,
        out_specs=pl.BlockSpec(memory_space=pl.ANY),
    )


def from_step(value, axis, step):
    count = lax.axis_size(axis)
    pairs = [(i, i + step) for i in range(count) if 0 <= i + step < count]
    return lax.ppermute(value, axis, pairs)


def swap(value, axis, starts):
    pairs = [(i, i + 1) for i in starts]
    return lax.ppermute(value, axis, pairs + [(j, i) for i, j in pairs])


def exchange(slab, place):
    depth, rows = lax.axis_size("gz"), lax.axis_size("gy")
    pairs = []
    for z in range(depth):
        for i, j in exchanges(rows - 1, z >= depth // 2)[place]:
            pairs.append((z * rows + i, z * rows + j))
    return lax.ppermute(slab, ("gz", "gy"), pairs)


def on_device(section, first_kernel, first_bias, second_kernel, second_bias, head_weight):
    own = section[0]
    columns, rows = lax.axis_size("gx"), lax.axis_size("gy")
    chip = swap(own, "gx", range(1, columns - 1, 2))
    core = swap(own, "gx", range(0, columns - 1, 2))
    given = (first_kernel, first_bias[None], second_kernel, second_bias[None], head_weight[None])
    weights = prepare(*given)
    side, *slabs = sides(own, core, chip, rows - 1)
    inside, slabs = inner_early(own, side, weights, slabs)
    borders = [exchange(slab, k) for k, slab in enumerate(slabs)]
    inside = inner(own, side, weights, inside)
    restored = outer(own, side, weights, inside, borders)
    across, down = dft_tables()
    later = from_step(restored, "gz", -1)
    spectrum = own_spectrum(restored, across, down)
    return cross_spectrum(later, across, down, spectrum)


def solution(mesh):
    placed = (P("gz", "gy", "gx"), P(), P(), P(), P(), P())
    return jax.shard_map(
        on_device, mesh=mesh, in_specs=placed, out_specs=P("gz", None, "gy", "gx"), check_vma=False
    )
```
